32 devices in a mesh: groups: 2 (over y), tm: 4 (over z), segment: 2 (over x), chan: 2 (over core).
Axes of the slice: x: 2, y: 2, z: 4, core: 2. Of those that a mesh axis runs over, the one named last changes fastest.
Arguments:
- records: bfloat16 [8, 1024, 256], P('groups', 'tm', 'chan'), parts along dimension 0, may hold values from -6 to 6
- conv_weight: bfloat16 [8, 512, 2, 256], P('segment', None, None, 'chan'), may hold values from -0.25 to 0.25
- conv_bias: bfloat16 [8, 2, 256], P('segment', None, 'chan'), may hold values from -3 to 3
- res_weight: bfloat16 [8, 256, 256], P('segment'), may hold values from -0.375 to 0.375
- skip_weight: bfloat16 [8, 256, 256], P('segment', None, 'chan'), may hold values from -0.375 to 0.375
Outputs:
- skip_out: bfloat16 [8, 1024, 256], P(('groups', 'segment'), 'tm', 'chan'), parts along dimension 0
The draws below stay inside these ranges and needn't reach their ends.
There are 2 independent parts, one for each index of `groups`. The reference program is written for one: setup_inputs(seed, part) draws one part's arguments, and reference() takes and returns one part's arrays. A program takes and returns all parts, laid end to end along the dimension named above; an argument that names none is the same for every part. Nothing has to cross between parts.
All inputs are finite; a program needn't handle non-finite values.
Results may differ from the reference program's by a relative error of at most 0.011.
Values may be sent and summed in bfloat16 or wider, within the bound.
No kernel may reach another device: no remote copies, remote signals or barrier semaphores. Data moves between devices by JAX's collectives and lax.ppermute only.
A program may use at most 64 MiB of HBM per device.

```python
import jax
import jax.numpy as jnp
from jax import lax

C = 256
SEG = 256
MB = 4
LPS = 4
LAYERS = 8
TIME = 1024
HOP_NEAR = 1
HOP_WIDE = 2


def block_scale(key, dims, shards, low, high):
    level, own = 1.0, jax.random.fold_in(key, 6)
    for position, parts in shards:
        steps = jnp.exp(jax.random.uniform(jax.random.fold_in(own, position), (parts,), jnp.float32, low / len(shards), high / len(shards)))
        level = level * jnp.repeat(steps, dims[position] // parts).reshape([-1 if axis == position else 1 for axis in range(len(dims))])
    return level


def scatter_about(rng, extent, spread, reach, cuts=(), kind=jnp.bfloat16):
    array = spread * jax.random.normal(rng, extent, jnp.float32)
    if cuts:
        array = array * block_scale(rng, extent, cuts, -0.22, 0.18)
    return jnp.clip(array, -reach, reach).astype(kind)


def setup_inputs(seed: int = 0, part: int = 0) -> dict:
    keys = jax.random.split(jax.random.key(seed), 6)
    part_splits = jax.random.split(jax.random.fold_in(keys[5], part), 6)
    records = scatter_about(part_splits[0], (MB, TIME, C), 1.0, 6.0, ((1, 4), (2, 2)))
    conv_weight = scatter_about(keys[1], (LAYERS, 2 * C, 2, C), (2 * C) ** -0.5, 0.25, ((0, 2), (3, 2)))
    conv_bias = scatter_about(keys[2], (LAYERS, 2, C), 0.5, 3.0, ((0, 2), (2, 2)))
    res_weight = scatter_about(keys[3], (LAYERS, C, C), C ** -0.5, 0.375, ((0, 2),))
    skip_weight = scatter_about(keys[4], (LAYERS, C, C), C ** -0.5, 0.375, ((0, 2), (2, 2)))
    return dict(records=records, conv_weight=conv_weight, conv_bias=conv_bias, res_weight=res_weight, skip_weight=skip_weight)


def run_record(record, conv_weight, conv_bias, res_weight, skip_weight):
    lag_sizes = [SEG // 8, SEG, SEG * HOP_NEAR, SEG * HOP_WIDE]
    stream = record
    skip_total = jnp.zeros((TIME, C), jnp.float32)
    for layer_no in range(LAYERS):
        lag_size = lag_sizes[layer_no % LPS]
        past_rows = jnp.concatenate([jnp.zeros((lag_size, C), stream.dtype), stream[:TIME - lag_size]], axis=0)
        conv_flat = conv_weight[layer_no].reshape(2 * C, 2 * C)
        pre_act = jnp.dot(past_rows, conv_flat[:C], preferred_element_type=jnp.float32)
        pre_act = pre_act + jnp.dot(stream, conv_flat[C:], preferred_element_type=jnp.float32)
        pre_act = pre_act + conv_bias[layer_no].reshape(2 * C).astype(jnp.float32)
        gate_out = (jnp.tanh(pre_act[:, :C]) * jax.nn.sigmoid(pre_act[:, C:])).astype(jnp.bfloat16)
        skip_total = skip_total + jnp.dot(gate_out, skip_weight[layer_no], preferred_element_type=jnp.float32)
        stream = (stream.astype(jnp.float32) + jnp.dot(gate_out, res_weight[layer_no], preferred_element_type=jnp.float32)).astype(jnp.bfloat16)
    return skip_total.astype(jnp.bfloat16)


def reference(records, conv_weight, conv_bias, res_weight, skip_weight):
    return lax.map(lambda record: run_record(record, conv_weight, conv_bias, res_weight, skip_weight), records)
```

```python
import functools

import jax
import jax.numpy as jnp
from jax import lax
from jax.experimental import pallas as pl
from jax.experimental.pallas import tpu as pltpu
from jax.sharding import PartitionSpec as P

VMEM = pl.BlockSpec(memory_space=pltpu.VMEM)
ROW_TILE = 256


def swap_cores(block):
    cores = lax.axis_size("chan")
    return lax.ppermute(block, "chan", [(i, cores - 1 - i) for i in range(cores)])


def section_body(own_pack, other_pack, res_ref, skip_ref, streams, units, lags, core):
    layers, depth = res_ref.shape[0], res_ref.shape[1]
    half = depth // 2
    head = max(lags)
    total = streams.shape[1] - head
    own_rows = pl.ds(pl.multiple_of(core * half, half), half)
    other_rows = pl.ds(pl.multiple_of((1 - core) * half, half), half)
    for layer in range(layers):
        now_buf, next_buf = streams.at[layer % 2], streams.at[(layer + 1) % 2]
        lag = lags[layer % 4]
        res = jnp.concatenate([res_ref[layer, own_rows, :], res_ref[layer, other_rows, :]], 0)

        def tile(row, lag=lag, layer=layer, now_buf=now_buf, next_buf=next_buf, res=res):
            past = now_buf[pl.ds(head - lag + row, ROW_TILE), :]
            now = now_buf[pl.ds(head + row, ROW_TILE), :]
            parts = []
            for pack in (own_pack, other_pack):
                pre = jnp.dot(past, pack[layer, :depth], preferred_element_type=jnp.float32)
                pre += jnp.dot(now, pack[layer, depth : 2 * depth], preferred_element_type=jnp.float32)
                pre += pack[layer, 2 * depth : 2 * depth + 1].astype(jnp.float32)
                gate = 0.5 * jnp.tanh(0.5 * pre[:, half:]) + 0.5
                parts.append((jnp.tanh(pre[:, :half]) * gate).astype(jnp.bfloat16))
            unit = jnp.concatenate(parts, 1)
            units[layer, pl.ds(row, ROW_TILE), :] = unit
            update = jnp.dot(unit, res, preferred_element_type=jnp.float32)
            next_buf[pl.ds(head + row, ROW_TILE), :] = (now.astype(jnp.float32) + update).astype(jnp.bfloat16)

        if total // ROW_TILE <= 4:
            for step in range(total // ROW_TILE):
                tile(step * ROW_TILE)
        else:
            pl.loop(0, total // ROW_TILE)(lambda step: tile(pl.multiple_of(step * ROW_TILE, ROW_TILE)))


def emit(skip_ref, streams, units, lags, core, first, skip_outs, stream_out, layers):
    half = skip_ref.shape[2]
    head = max(lags)
    total = streams.shape[1] - head
    own_rows = pl.ds(pl.multiple_of(core * half, half), half)
    other_rows = pl.ds(pl.multiple_of((1 - core) * half, half), half)
    rows = skip_outs[0].shape[0]
    blocks = total // rows
    for turn, out in enumerate(skip_outs):
        at = pl.multiple_of(lax.rem(first + turn, blocks) * rows, rows)
        acc = jnp.zeros((rows, half), jnp.float32)
        for layer in range(layers):
            unit = units[layer, pl.ds(at, rows), :]
            acc += jnp.dot(unit[:, :half], skip_ref[layer, own_rows, :], preferred_element_type=jnp.float32)
            acc += jnp.dot(unit[:, half:], skip_ref[layer, other_rows, :], preferred_element_type=jnp.float32)
        out[...] = acc.astype(out.dtype)
    if stream_out is not None:
        part = total // 2
        start = pl.multiple_of(head + core * part, 16)
        stream_out[...] = streams[layers % 2, pl.ds(start, part), :]


def section_kernel(stage, shift, lags, n_in, n_skip, has_stream, *refs):
    own_pack, other_pack, res_ref, skip_ref = refs[:4]
    inputs = refs[4 : 4 + n_in]
    skip_outs = refs[4 + n_in : 4 + n_in + n_skip]
    stream_out = refs[4 + n_in + n_skip] if has_stream else None
    streams, units = refs[-2:]
    core, place = lax.axis_index("chan"), lax.axis_index("tm")
    count = lax.axis_size("tm")
    head = max(lags)
    layers = res_ref.shape[0]
    half = skip_ref.shape[2]

    @pl.when(lax.axis_index("segment") == stage)
    def _():
        streams[:, :head, :] = jnp.zeros((2, head, streams.shape[2]), streams.dtype)
        if stage == 0:
            rows = inputs[0].shape[0]
            for side, blocks in ((core, inputs[: n_in // 2]), (1 - core, inputs[n_in // 2 :])):
                lanes = pl.ds(pl.multiple_of(side * half, half), half)
                for turn, block in enumerate(blocks):
                    at = lax.rem(place - turn + count, count) * rows + head
                    streams[0, pl.ds(pl.multiple_of(at, 16), rows), lanes] = block[...]
        else:
            part = inputs[0].shape[0]
            for side, block in ((core, inputs[0]), (1 - core, inputs[1])):
                streams[0, pl.ds(pl.multiple_of(head + side * part, 16), part), :] = block[...]
        section_body(own_pack, other_pack, res_ref, skip_ref, streams, units, lags, core)
        emit(skip_ref, streams, units, lags, core, place + shift, skip_outs, stream_out, layers)


def run_section(stage, last, shift, lags, packs, res_weight, skip_weight, inputs, rows, n_skip):
    layers, depth = res_weight.shape[:2]
    total = rows * lax.axis_size("tm")
    half = skip_weight.shape[2]
    outs = [jax.ShapeDtypeStruct((rows, half), jnp.bfloat16)] * n_skip
    if not last:
        outs.append(jax.ShapeDtypeStruct((total // 2, depth), jnp.bfloat16))
    scratch = [
        pltpu.VMEM((2, max(lags) + total, depth), jnp.bfloat16),
        pltpu.VMEM((layers, total, depth), jnp.bfloat16),
    ]
    held = 2 * (2 * (max(lags) + total) * depth + layers * total * depth + 2 * total * depth)
    return pl.pallas_call(
        functools.partial(section_kernel, stage, shift, lags, len(inputs), n_skip, not last),
        out_shape=outs,
        in_specs=[VMEM] * (4 + len(inputs)),
        out_specs=[VMEM] * len(outs),
        scratch_shapes=scratch,
        compiler_params=pltpu.CompilerParams(vmem_limit_bytes=held + (14 << 20)),
    )(*packs, res_weight, skip_weight, *inputs)


def shards(records, conv_weight, conv_bias, res_weight, skip_weight):
    record_count, rows, half = records.shape
    layers, taps = conv_weight.shape[:2]
    count, sections = lax.axis_size("tm"), lax.axis_size("segment")
    place, segment = lax.axis_index("tm"), lax.axis_index("segment")
    lags = [rows // 8, rows, rows * max(1, count // 8), rows * max(1, count // 2)]
    share = record_count // sections

    own_blocks = []
    for turn in range(count):
        slot = lax.rem(lax.rem(place + turn, count), record_count)
        block = lax.dynamic_index_in_dim(records, slot, 0, keepdims=False)
        if turn:
            block = lax.ppermute(block, "tm", [(i, (i + turn) % count) for i in range(count)])
        own_blocks.append(block)
    other_blocks = [swap_cores(block) for block in own_blocks]

    bias_rows = jnp.pad(conv_bias.reshape(layers, 1, 2 * half), ((0, 0), (0, 15), (0, 0)))
    own_pack = jnp.concatenate([conv_weight.reshape(layers, taps, 2 * half), bias_rows], 1)
    packs = (own_pack, swap_cores(own_pack))

    inputs = own_blocks + other_blocks
    skip_parts = None
    for stage in range(sections):
        last = stage == sections - 1
        outs = run_section(stage, last, stage * share, lags, packs, res_weight, skip_weight, inputs, rows, record_count)
        blocks = outs[:record_count]
        if skip_parts is None:
            skip_parts = blocks
        else:
            skip_parts = [jnp.where(segment == stage, new, old) for new, old in zip(blocks, skip_parts)]
        if not last:
            moved = lax.ppermute(outs[-1], "segment", [(i, (i + 1) % sections) for i in range(sections)])
            inputs = [moved, swap_cores(moved)]

    result = jnp.zeros((share, rows, half), jnp.float32)
    first = segment * share
    for turn in range(record_count):
        pairs = []
        for z in range(count):
            for s in range(sections):
                to = (z + turn + s * share) % count
                pairs.append((z * sections + s, to * sections + (z % record_count) // share))
        got = lax.ppermute(skip_parts[turn], ("tm", "segment"), pairs)
        for s in range(sections):
            source = lax.rem(lax.rem(place - turn - s * share + 2 * count, count), record_count)
            inside = jnp.logical_and(source >= first, source < first + share)
            for j in range(share):
                mine = jnp.logical_and(inside, source - first == j)
                result = result.at[j].add(jnp.where(mine, got.astype(jnp.float32), 0.0))
    return result.astype(jnp.bfloat16)


def solution(mesh):
    return jax.shard_map(
        shards,
        mesh=mesh,
        in_specs=(
            P("groups", "tm", "chan"),
            P("segment", None, None, "chan"),
            P("segment", None, "chan"),
            P("segment", None, None),
            P("segment", None, "chan"),
        ),
        out_specs=P(("groups", "segment"), "tm", "chan"),
        check_vma=False,
    )
```

```python
import functools

import jax
import jax.numpy as jnp
from jax import lax
from jax.experimental import pallas as pl
from jax.experimental.pallas import tpu as pltpu
from jax.sharding import PartitionSpec as P

VMEM = pl.BlockSpec(memory_space=pltpu.VMEM)
ROW_TILE = 256


class Plan:
    def __init__(self, count, sections, records):
        self.count, self.sections, self.records = count, sections, records
        self.share = records // sections
        self.whole_group = records <= count // 2
        self.blocks = records // 2 if self.whole_group else max(1, records // 4)

    def owner(self, z):
        return z % self.records % self.sections

    def slot(self, z):
        return z % self.records // self.sections

    def record_at(self, z):
        return self.owner(z) * self.share + self.slot(z)

    def time_block(self, z, core, half, index):
        if self.whole_group:
            return z // self.records * self.records + 2 * index + core
        return half * (self.count // 2) + 2 * index + core

    def landing_core(self, segment, half, slot):
        return (slot + half + segment + 1) % 2

    def transfers(self, stage, half, index):
        sends = {}
        for z in range(self.count):
            for core in range(2):
                t = self.time_block(z, core, half, index)
                if t // (self.count // 2) == half:
                    to = self.owner(z)
                    sends[z, stage, core] = (t, to, self.landing_core(to, half, self.slot(z)))
        return sends


def complete(sends, shape):
    devices = [(z, s, c) for z in range(shape[0]) for s in range(shape[1]) for c in range(shape[2])]
    taken = set(sends.values())
    sources = [d for d in devices if d not in sends]
    targets = [d for d in devices if d not in taken]
    pairs = dict(sends)

    def near(pair):
        a, b = pair
        return (a == b, abs(a[0] - b[0]), a[1] != b[1])

    for source in sources:
        target = min(targets, key=lambda b: near((source, b)))
        targets.remove(target)
        pairs[source] = target
    for a in [d for d in sources if pairs[d] == d]:
        b = next((d for d in sources if d != a and pairs[d] != a), None)
        if b is not None:
            pairs[a], pairs[b] = pairs[b], pairs[a]
    return pairs


def swap_cores(block):
    return lax.ppermute(block, "chan", [(0, 1), (1, 0)])


def section_kernel(stage, half, plan, lags, n_in, last, *refs):
    own_pack, other_pack, res_ref, own_skip, other_skip = refs[:5]
    inputs, refs = refs[5 : 5 + n_in], refs[5 + n_in :]
    layers, depth = res_ref.shape[:2]
    width = depth // 2
    heads = ()
    if half:
        heads, refs = refs[:layers], refs[layers:]
    skip_outs, refs = refs[: plan.blocks], refs[plan.blocks :]
    if not last:
        stream_out, refs = refs[0], refs[1:]
    if not half:
        tails, refs = refs[:layers], refs[layers:]
    streams, units, out_buf = refs[:layers], refs[layers], refs[layers + 1]
    core, place = lax.axis_index("chan"), lax.axis_index("tm")
    total = units.shape[1]
    own_rows = pl.ds(pl.multiple_of(core * width, width), width)
    other_rows = pl.ds(pl.multiple_of((1 - core) * width, width), width)

    @pl.when(lax.axis_index("segment") == stage)
    def _():
        for layer in range(layers):
            lag = lags[layer % 4]
            streams[layer][:lag, :] = heads[layer][...] if half else jnp.zeros((lag, depth), jnp.bfloat16)
        if stage == 0:
            rows = inputs[0].shape[0]
            per_half = plan.count // 2
            for side, blocks in ((own_rows, inputs[: n_in // 2]), (other_rows, inputs[n_in // 2 :])):
                for turn, block in enumerate(blocks):
                    t = lax.rem(place - turn + plan.count, plan.count)

                    @pl.when(t // per_half == half)
                    def _(t=t, block=block, side=side):
                        at = pl.multiple_of(lags[0] + (t - half * per_half) * rows, 16)
                        streams[0][pl.ds(at, rows), side] = block[...]
        else:
            part = inputs[0].shape[0]
            for side, block in ((core, inputs[0]), (1 - core, inputs[1])):
                streams[0][pl.ds(pl.multiple_of(lags[0] + side * part, 16), part), :] = block[...]

        for layer in range(layers):
            lag = lags[layer % 4]
            now_buf = streams[layer]
            next_buf, next_lag = (streams[layer + 1], lags[(layer + 1) % 4]) if layer + 1 < layers else (out_buf, 0)
            res = None
            if not (last and layer + 1 == layers):
                res = jnp.concatenate([res_ref[layer, own_rows, :], res_ref[layer, other_rows, :]], 0)

            def tile(row, layer=layer, lag=lag, now_buf=now_buf, next_buf=next_buf, next_lag=next_lag, res=res):
                past = now_buf[pl.ds(row, ROW_TILE), :]
                now = now_buf[pl.ds(lag + row, ROW_TILE), :]
                parts = []
                for pack in (own_pack, other_pack):
                    pre = jnp.dot(past, pack[layer, :depth], preferred_element_type=jnp.float32)
                    pre += jnp.dot(now, pack[layer, depth : 2 * depth], preferred_element_type=jnp.float32)
                    pre += pack[layer, 2 * depth : 2 * depth + 1].astype(jnp.float32)
                    gate = 0.5 * jnp.tanh(0.5 * pre[:, width:]) + 0.5
                    parts.append((jnp.tanh(pre[:, :width]) * gate).astype(jnp.bfloat16))
                unit = jnp.concatenate(parts, 1)
                units[layer, pl.ds(row, ROW_TILE), :] = unit
                if res is not None:
                    update = jnp.dot(unit, res, preferred_element_type=jnp.float32)
                    next_buf[pl.ds(next_lag + row, ROW_TILE), :] = (now.astype(jnp.float32) + update).astype(jnp.bfloat16)

            steps = total // ROW_TILE
            if steps <= 4:
                for step in range(steps):
                    tile(step * ROW_TILE)
            else:
                pl.loop(0, steps)(lambda step: tile(pl.multiple_of(step * ROW_TILE, ROW_TILE)))

        if not last:
            part = total // 2
            stream_out[...] = out_buf[pl.ds(pl.multiple_of(core * part, 16), part), :]
        if not half:
            for layer in range(layers):
                tails[layer][...] = streams[layer][pl.ds(total, lags[layer % 4]), :]
        for index, out in enumerate(skip_outs):
            rows = out.shape[0]
            t = plan.time_block(place, core, half, index) - half * (plan.count // 2)
            at = pl.multiple_of(jnp.clip(t, 0, total // rows - 1) * rows, rows)
            acc = jnp.zeros((rows, depth), jnp.float32)
            for layer in range(layers):
                unit = units[layer, pl.ds(at, rows), :]
                skip = jnp.concatenate(
                    [
                        jnp.concatenate([part[layer, own_rows, :], part[layer, other_rows, :]], 0)
                        for part in (own_skip, other_skip)
                    ],
                    1,
                )
                acc += jnp.dot(unit, skip, preferred_element_type=jnp.float32)
            out[:, own_rows] = acc[:, :width].astype(out.dtype)
            out[:, other_rows] = acc[:, width:].astype(out.dtype)


def run_section(stage, half, plan, lags, weights, inputs, heads, rows):
    res_weight = weights[2]
    layers, depth = res_weight.shape[:2]
    total = rows * plan.count // 2
    last = stage == plan.sections - 1
    outs = [jax.ShapeDtypeStruct((rows, depth), jnp.bfloat16)] * plan.blocks
    if not last:
        outs.append(jax.ShapeDtypeStruct((total // 2, depth), jnp.bfloat16))
    if not half:
        outs += [jax.ShapeDtypeStruct((lags[layer % 4], depth), jnp.bfloat16) for layer in range(layers)]
    scratch = [pltpu.VMEM((lags[layer % 4] + total, depth), jnp.bfloat16) for layer in range(layers)]
    scratch += [pltpu.VMEM((layers, total, depth), jnp.bfloat16), pltpu.VMEM((total, depth), jnp.bfloat16)]
    held = 2 * depth * (sum(lags) * 3 + 13 * total)
    got = pl.pallas_call(
        functools.partial(section_kernel, stage, half, plan, lags, len(inputs), last),
        out_shape=outs,
        in_specs=[VMEM] * (len(weights) + len(inputs) + len(heads)),
        out_specs=[VMEM] * len(outs),
        scratch_shapes=scratch,
        compiler_params=pltpu.CompilerParams(vmem_limit_bytes=held + (12 << 20)),
    )(*weights, *inputs, *heads)
    blocks, got = got[: plan.blocks], got[plan.blocks :]
    stream = None
    if not last:
        stream, got = got[0], got[1:]
    return blocks, stream, got


def shards(records, conv_weight, conv_bias, res_weight, skip_weight):
    record_count, rows, width = records.shape
    layers, taps = conv_weight.shape[:2]
    count, sections = lax.axis_size("tm"), lax.axis_size("segment")
    place, segment, core = lax.axis_index("tm"), lax.axis_index("segment"), lax.axis_index("chan")
    lags = [rows // 8, rows, rows * max(1, count // 8), rows * max(1, count // 2)]
    plan = Plan(count, sections, record_count)

    own_blocks = []
    for turn in range(count):
        block = lax.dynamic_index_in_dim(records, plan.record_at(lax.rem(place + turn, count)), 0, keepdims=False)
        if turn:
            block = lax.ppermute(block, "tm", [(i, (i + turn) % count) for i in range(count)])
        own_blocks.append(block)
    inputs = own_blocks + [swap_cores(block) for block in own_blocks]

    bias_rows = jnp.pad(conv_bias.reshape(layers, 1, 2 * width), ((0, 0), (0, 15), (0, 0)))
    own_pack = jnp.concatenate([conv_weight.reshape(layers, taps, 2 * width), bias_rows], 1)
    weights = (own_pack, swap_cores(own_pack), res_weight, skip_weight, swap_cores(skip_weight))

    skips = {}
    fed = [inputs, inputs]
    for stage in range(sections):
        heads, crossed = (), []
        for half in range(2):
            skips[stage, half], stream, carried = run_section(
                stage, half, plan, lags, weights, fed[half], heads, rows
            )
            heads = carried
            if stage < sections - 1:
                moved = lax.ppermute(stream, "segment", [(i, (i + 1) % sections) for i in range(sections)])
                crossed.append([moved, swap_cores(moved)])
        fed = crossed

    total = jnp.zeros((rows, 2 * width), jnp.float32)
    spot = (place * sections + segment) * 2 + core
    for early in (True, False):
        for index in range(plan.blocks):
            groups = []
            for stage in reversed(range(sections)):
                half = int((stage == sections - 1) != early)
                sends = plan.transfers(stage, half, index)
                for group in groups:
                    if not set(group[0].values()) & set(sends.values()):
                        group[0].update(sends)
                        group[1].append((stage, half))
                        break
                else:
                    groups.append((sends, [(stage, half)]))
            for sends, members in groups:
                payload = None
                for stage, half in members:
                    block = skips[stage, half][index]
                    payload = block if payload is None else jnp.where(segment == stage, block, payload)
                pairs = complete(sends, (count, sections, 2))
                number = lambda d: (d[0] * sections + d[1]) * 2 + d[2]
                got = lax.ppermute(
                    payload, ("tm", "segment", "chan"), sorted((number(a), number(b)) for a, b in pairs.items())
                )
                valid = functools.reduce(jnp.logical_or, [spot == number(d) for d in sends.values()])
                if len(sends) == 2 * count * sections:
                    total = total + got.astype(jnp.float32)
                else:
                    total = total + jnp.where(valid, got.astype(jnp.float32), 0.0)
    block = total.astype(jnp.bfloat16)
    low, high = block[:, :width], block[:, width:]
    kept = jnp.where(core == 0, low, high)
    given = swap_cores(jnp.where(core == 0, high, low))
    mine = lax.rem(core + place // (count // 2) + segment + 1, 2)
    return jnp.stack([jnp.where(mine == slot, kept, given) for slot in range(plan.share)])


def solution(mesh):
    return jax.shard_map(
        shards,
        mesh=mesh,
        in_specs=(
            P("groups", "tm", "chan"),
            P("segment", None, None, "chan"),
            P("segment", None, "chan"),
            P("segment", None, None),
            P("segment", None, "chan"),
        ),
        out_specs=P(("groups", "segment"), "tm", "chan"),
        check_vma=False,
    )
```

```python
import functools

import jax
import jax.numpy as jnp
from jax import lax
from jax.experimental import pallas as pl
from jax.experimental.pallas import tpu as pltpu
from jax.sharding import PartitionSpec as P

VMEM = pl.BlockSpec(memory_space=pltpu.VMEM)
ROW_TILE = 256


class Plan:
    def __init__(self, count, sections, records):
        self.count, self.sections, self.records = count, sections, records
        self.share = records // sections
        self.whole_group = records <= count // 2
        self.blocks = records // 2 if self.whole_group else max(1, records // 4)

    def owner(self, z):
        return z % self.records % self.sections

    def slot(self, z):
        return z % self.records // self.sections

    def record_at(self, z):
        return self.owner(z) * self.share + self.slot(z)

    def time_block(self, z, core, half, index):
        if self.whole_group:
            return z // self.records * self.records + 2 * index + core
        return half * (self.count // 2) + 2 * index + core

    def landing_core(self, segment, half, slot):
        return (slot + half + segment + 1) % 2

    def turned(self, z, turn):
        return lax.bitwise_xor(z, turn)

    def trade_pairs(self, turn):
        pairs = []
        for z in range(self.count):
            for s in range(self.sections):
                to = (z ^ turn, s)
                if turn == self.count - 1 and s < 2 <= self.sections:
                    to = (z, 1) if s == 0 else (z ^ turn, 0)
                pairs.append((z * self.sections + s, to[0] * self.sections + to[1]))
        return pairs

    def leave_groups(self, early, index):
        groups = []
        for stage in reversed(range(self.sections)):
            half = int((stage == self.sections - 1) != early)
            sends = self.transfers(stage, half, index)
            for known, members in groups:
                if not set(known.values()) & set(sends.values()):
                    known.update(sends)
                    members.append((stage, half))
                    break
            else:
                groups.append((sends, [(stage, half)]))
        return groups

    def transfers(self, stage, half, index):
        sends = {}
        for z in range(self.count):
            for core in range(2):
                t = self.time_block(z, core, half, index)
                if t // (self.count // 2) == half:
                    to = self.owner(z)
                    sends[z, stage, core] = (t, to, self.landing_core(to, half, self.slot(z)))
        return sends


def complete(sends, shape):
    devices = [(z, s, c) for z in range(shape[0]) for s in range(shape[1]) for c in range(shape[2])]
    taken = set(sends.values())
    sources = [d for d in devices if d not in sends]
    targets = [d for d in devices if d not in taken]
    pairs = dict(sends)

    def near(pair):
        a, b = pair
        return (a == b, abs(a[0] - b[0]), a[1] != b[1])

    for source in sources:
        target = min(targets, key=lambda b: near((source, b)))
        targets.remove(target)
        pairs[source] = target
    for a in [d for d in sources if pairs[d] == d]:
        b = next((d for d in sources if d != a and pairs[d] != a), None)
        if b is not None:
            pairs[a], pairs[b] = pairs[b], pairs[a]
    return pairs


def swap_cores(block):
    return lax.ppermute(block, "chan", [(0, 1), (1, 0)])


def section_kernel(stage, half, plan, lags, n_in, n_earlier, last, *refs):
    own_conv, other_conv, own_bias, other_bias, res_ref, own_skip, other_skip = refs[:7]
    inputs, refs = refs[7 : 7 + n_in], refs[7 + n_in :]
    layers, depth = res_ref.shape[:2]
    width = depth // 2
    heads = ()
    if half:
        heads, refs = refs[:layers], refs[layers:]
    earlier, refs = refs[:n_earlier], refs[n_earlier:]
    skip_outs, refs = refs[: plan.blocks], refs[plan.blocks :]
    if not last:
        stream_out, refs = refs[0], refs[1:]
    if not half:
        tails, refs = refs[:layers], refs[layers:]
    streams, units, out_buf = refs[:layers], refs[layers], refs[layers + 1]
    core, place = lax.axis_index("chan"), lax.axis_index("tm")
    total = units.shape[1]
    own_rows = pl.ds(pl.multiple_of(core * width, width), width)
    other_rows = pl.ds(pl.multiple_of((1 - core) * width, width), width)

    if earlier:

        @pl.when(lax.axis_index("segment") != stage)
        def _():
            for block, out in zip(earlier, skip_outs):
                out[...] = block[...]

    @pl.when(lax.axis_index("segment") == stage)
    def _():
        for layer in range(layers):
            lag = lags[layer % 4]
            streams[layer][:lag, :] = heads[layer][...] if half else jnp.zeros((lag, depth), jnp.bfloat16)
        if stage == 0:
            rows = inputs[0].shape[0]
            per_half = plan.count // 2
            for side, blocks in ((own_rows, inputs[: n_in // 2]), (other_rows, inputs[n_in // 2 :])):
                for turn, block in enumerate(blocks):
                    t = plan.turned(place, turn)

                    @pl.when(t // per_half == half)
                    def _(t=t, block=block, side=side):
                        at = pl.multiple_of(lags[0] + (t - half * per_half) * rows, 16)
                        streams[0][pl.ds(at, rows), side] = block[...]
        else:
            part = inputs[0].shape[0]
            for side, block in ((core, inputs[0]), (1 - core, inputs[1])):
                streams[0][pl.ds(pl.multiple_of(lags[0] + side * part, 16), part), :] = block[...]

        for layer in range(layers):
            lag = lags[layer % 4]
            now_buf = streams[layer]
            next_buf, next_lag = (streams[layer + 1], lags[(layer + 1) % 4]) if layer + 1 < layers else (out_buf, 0)
            res = None
            if not (last and layer + 1 == layers):
                res = jnp.concatenate([res_ref[layer, own_rows, :], res_ref[layer, other_rows, :]], 0)

            def tile(row, layer=layer, lag=lag, now_buf=now_buf, next_buf=next_buf, next_lag=next_lag, res=res):
                past = now_buf[pl.ds(row, ROW_TILE), :]
                now = now_buf[pl.ds(lag + row, ROW_TILE), :]
                parts = []
                for conv, bias in ((own_conv, own_bias), (other_conv, other_bias)):
                    shift = jnp.concatenate([bias[layer, 0:1, :], bias[layer, 1:2, :]], 1).astype(jnp.float32)
                    pre = jnp.dot(past, conv[layer, :depth], preferred_element_type=jnp.float32)
                    pre += jnp.dot(now, conv[layer, depth:], preferred_element_type=jnp.float32)
                    pre += shift
                    gate = 0.5 * jnp.tanh(0.5 * pre[:, width:]) + 0.5
                    parts.append((jnp.tanh(pre[:, :width]) * gate).astype(jnp.bfloat16))
                unit = jnp.concatenate(parts, 1)
                units[layer, pl.ds(row, ROW_TILE), :] = unit
                if res is not None:
                    update = jnp.dot(unit, res, preferred_element_type=jnp.float32)
                    next_buf[pl.ds(next_lag + row, ROW_TILE), :] = (now.astype(jnp.float32) + update).astype(jnp.bfloat16)

            steps = total // ROW_TILE
            if steps <= 4:
                for step in range(steps):
                    tile(step * ROW_TILE)
            else:
                pl.loop(0, steps)(lambda step: tile(pl.multiple_of(step * ROW_TILE, ROW_TILE)))

        if not last:
            part = total // 2
            stream_out[...] = out_buf[pl.ds(pl.multiple_of(core * part, 16), part), :]
        if not half:
            for layer in range(layers):
                tails[layer][...] = streams[layer][pl.ds(total, lags[layer % 4]), :]
        for index, out in enumerate(skip_outs):
            rows = out.shape[0]
            t = plan.time_block(place, core, half, index) - half * (plan.count // 2)
            at = pl.multiple_of(jnp.clip(t, 0, total // rows - 1) * rows, rows)
            acc = jnp.zeros((rows, depth), jnp.float32)
            for layer in range(layers):
                unit = units[layer, pl.ds(at, rows), :]
                skip = jnp.concatenate(
                    [
                        jnp.concatenate([part[layer, own_rows, :], part[layer, other_rows, :]], 0)
                        for part in (own_skip, other_skip)
                    ],
                    1,
                )
                acc += jnp.dot(unit, skip, preferred_element_type=jnp.float32)
            out[:, own_rows] = acc[:, :width].astype(out.dtype)
            out[:, other_rows] = acc[:, width:].astype(out.dtype)


def run_section(stage, half, plan, lags, weights, inputs, heads, earlier, rows):
    res_weight = weights[4]
    layers, depth = res_weight.shape[:2]
    total = rows * plan.count // 2
    last = stage == plan.sections - 1
    outs = [jax.ShapeDtypeStruct((rows, depth), jnp.bfloat16)] * plan.blocks
    if not last:
        outs.append(jax.ShapeDtypeStruct((total // 2, depth), jnp.bfloat16))
    if not half:
        outs += [jax.ShapeDtypeStruct((lags[layer % 4], depth), jnp.bfloat16) for layer in range(layers)]
    scratch = [pltpu.VMEM((lags[layer % 4] + total, depth), jnp.bfloat16) for layer in range(layers)]
    scratch += [pltpu.VMEM((layers, total, depth), jnp.bfloat16), pltpu.VMEM((total, depth), jnp.bfloat16)]
    held = 2 * depth * (sum(lags) * 3 + 13 * total)
    got = pl.pallas_call(
        functools.partial(section_kernel, stage, half, plan, lags, len(inputs), len(earlier), last),
        out_shape=outs,
        in_specs=[VMEM] * (len(weights) + len(inputs) + len(heads) + len(earlier)),
        out_specs=[VMEM] * len(outs),
        scratch_shapes=scratch,
        compiler_params=pltpu.CompilerParams(vmem_limit_bytes=held + (12 << 20)),
        cost_estimate=pl.CostEstimate(flops=16 * total * depth * depth * layers, bytes_accessed=1 << 20, transcendentals=0),
    )(*weights, *inputs, *heads, *earlier)
    blocks, got = got[: plan.blocks], got[plan.blocks :]
    stream = None
    if not last:
        stream, got = got[0], got[1:]
    return blocks, stream, got


def shards(records, conv_weight, conv_bias, res_weight, skip_weight):
    record_count, rows, width = records.shape
    layers, taps = conv_weight.shape[:2]
    count, sections = lax.axis_size("tm"), lax.axis_size("segment")
    place, segment, core = lax.axis_index("tm"), lax.axis_index("segment"), lax.axis_index("chan")
    lags = [rows // 8, rows, rows * max(1, count // 8), rows * max(1, count // 2)]
    plan = Plan(count, sections, record_count)

    blocks = [
        lax.dynamic_index_in_dim(records, plan.record_at(plan.turned(place, turn)), 0, keepdims=False)
        for turn in range(count)
    ]
    for turn in range(1, count):
        blocks[turn] = lax.ppermute(blocks[turn], ("tm", "segment"), plan.trade_pairs(turn))
    conv = conv_weight.reshape(layers, taps, 2 * width)
    weights = (conv, swap_cores(conv), conv_bias, swap_cores(conv_bias), res_weight, skip_weight, swap_cores(skip_weight))
    inputs = blocks + [swap_cores(block) for block in blocks]

    skips = {}
    fed = [inputs, inputs]
    for stage in range(sections):
        heads, crossed = (), []
        for half in range(2):
            earlier = []
            if stage == sections - 1:
                for index in range(plan.blocks):
                    members = plan.leave_groups(half == 0, index)[0][1][1:]
                    if members:
                        block = skips[members[0]][index]
                        for member in members[1:]:
                            block = jnp.where(segment == member[0], skips[member][index], block)
                        earlier.append(block)
                earlier = earlier if len(earlier) == plan.blocks else []
            came = fed[half]
            if stage:
                if half:
                    came, heads = lax.optimization_barrier((came, heads))
                else:
                    came, stream = lax.optimization_barrier((came, stream))
                came = [came, swap_cores(came)]
            skips[stage, half], stream, carried = run_section(
                stage, half, plan, lags, weights, came, heads, earlier, rows
            )
            heads = carried
            if stage < sections - 1:
                moved = lax.ppermute(stream, "segment", [(i, (i + 1) % sections) for i in range(sections)])
                crossed.append(moved)
        fed = crossed

    arrived, holds = [], []
    spot = (place * sections + segment) * 2 + core

    def number(device):
        return (device[0] * sections + device[1]) * 2 + device[2]

    for early in (True, False):
        for index in range(plan.blocks):
            for sends, members in plan.leave_groups(early, index):
                payload = skips[members[0]][index]
                if members[0][0] != sections - 1:
                    for member in members[1:]:
                        payload = jnp.where(segment == member[0], skips[member][index], payload)
                pairs = complete(sends, (count, sections, 2))
                arrived.append(
                    lax.ppermute(
                        payload, ("tm", "segment", "chan"), sorted((number(a), number(b)) for a, b in pairs.items())
                    )
                )
                valid = jnp.bool_(True)
                if len(sends) < 2 * count * sections:
                    valid = functools.reduce(jnp.logical_or, [spot == number(d) for d in sends.values()])
                holds.append(valid.astype(jnp.int32))
    kept, given = pl.pallas_call(
        functools.partial(sum_kernel, len(arrived)),
        out_shape=[jax.ShapeDtypeStruct((rows, width), jnp.bfloat16)] * 2,
        in_specs=[pl.BlockSpec(memory_space=pltpu.SMEM)] + [VMEM] * len(arrived),
        out_specs=[VMEM] * 2,
        compiler_params=pltpu.CompilerParams(vmem_limit_bytes=4 << 20),
    )(jnp.stack(holds), *arrived)
    return pl.pallas_call(
        functools.partial(place_kernel, plan),
        out_shape=jax.ShapeDtypeStruct((plan.share, rows, width), jnp.bfloat16),
        in_specs=[VMEM] * 2,
        out_specs=VMEM,
        compiler_params=pltpu.CompilerParams(vmem_limit_bytes=4 << 20),
    )(kept, swap_cores(given))


def sum_kernel(count, holds, *refs):
    arrived, (kept, given) = refs[:count], refs[count:]
    width = kept.shape[1]
    core = lax.axis_index("chan")
    for side, out in ((core, kept), (1 - core, given)):
        lanes = pl.ds(pl.multiple_of(side * width, width), width)
        total = jnp.zeros(out.shape, jnp.float32)
        for index, block in enumerate(arrived):
            total += jnp.where(holds[index] == 1, block[:, lanes].astype(jnp.float32), 0.0)
        out[...] = total.astype(out.dtype)


def place_kernel(plan, kept, given, out):
    half = lax.axis_index("tm") // (plan.count // 2)
    mine = lax.rem(lax.axis_index("chan") + half + lax.axis_index("segment") + 1, 2)
    for slot in range(plan.share):
        out[slot] = jnp.where(mine == slot, kept[...], given[...])


def solution(mesh):
    return jax.shard_map(
        shards,
        mesh=mesh,
        in_specs=(
            P("groups", "tm", "chan"),
            P("segment", None, None, "chan"),
            P("segment", None, "chan"),
            P("segment", None, None),
            P("segment", None, "chan"),
        ),
        out_specs=P(("groups", "segment"), "tm", "chan"),
        check_vma=False,
    )
```

```python
import functools

import jax
import jax.numpy as jnp
from jax import lax
from jax.experimental import pallas as pl
from jax.experimental.pallas import tpu as pltpu
from jax.sharding import PartitionSpec as P

VMEM = pl.BlockSpec(memory_space=pltpu.VMEM)
ROW_TILE = 256
PIECES = 2


class Plan:
    def __init__(self, count, sections, records):
        self.count, self.sections, self.records = count, sections, records
        self.share = records // sections
        self.whole_group = records <= count // 2
        self.blocks = records // 2 if self.whole_group else max(1, records // 4)

    def owner(self, z):
        return z % self.records % self.sections

    def slot(self, z):
        return z % self.records // self.sections

    def record_at(self, z):
        return self.owner(z) * self.share + self.slot(z)

    def time_block(self, z, core, half, index):
        if self.whole_group:
            return z // self.records * self.records + 2 * index + core
        return half * (self.count // 2) + 2 * index + core

    def landing_core(self, segment, half, slot):
        return (slot + half + segment + 1) % 2

    def from_chip(self, z, turn):
        return lax.rem(z - turn + self.count, self.count)

    def leave_groups(self, phase, index):
        groups = []
        for stage in reversed(range(self.sections)):
            half = phase if stage == self.sections - 1 else 1 - phase
            sends = self.transfers(stage, half, index)
            for known, members in groups:
                if not set(known.values()) & set(sends.values()):
                    known.update(sends)
                    members.append((stage, half))
                    break
            else:
                groups.append((sends, [(stage, half)]))
        return groups

    def transfers(self, stage, half, index):
        sends = {}
        for z in range(self.count):
            for core in range(2):
                t = self.time_block(z, core, half, index)
                if t // (self.count // 2) == half:
                    to = self.owner(z)
                    sends[z, stage, core] = (t, to, self.landing_core(to, half, self.slot(z)))
        return sends


def complete(sends, shape):
    devices = [(z, s, c) for z in range(shape[0]) for s in range(shape[1]) for c in range(shape[2])]
    taken = set(sends.values())
    sources = [d for d in devices if d not in sends]
    targets = [d for d in devices if d not in taken]
    pairs = dict(sends)

    def near(pair):
        a, b = pair
        return (a == b, abs(a[0] - b[0]), a[1] != b[1])

    for source in sources:
        target = min(targets, key=lambda b: near((source, b)))
        targets.remove(target)
        pairs[source] = target
    for a in [d for d in sources if pairs[d] == d]:
        b = next((d for d in sources if d != a and pairs[d] != a), None)
        if b is not None:
            pairs[a], pairs[b] = pairs[b], pairs[a]
    return pairs


def swap_cores(block):
    return lax.ppermute(block, "chan", [(0, 1), (1, 0)])


def section_kernel(stage, half, plan, lags, n_in, n_earlier, last, *refs):
    own_conv, other_conv, own_bias, other_bias, res_ref, own_skip, other_skip = refs[:7]
    inputs, refs = refs[7 : 7 + n_in], refs[7 + n_in :]
    layers, depth = res_ref.shape[:2]
    width = depth // 2
    heads = ()
    if half:
        heads, refs = refs[:layers], refs[layers:]
    earlier, refs = refs[:n_earlier], refs[n_earlier:]
    skip_outs, refs = refs[: plan.blocks], refs[plan.blocks :]
    if not last:
        stream_out, refs = refs[0], refs[1:]
    if not half:
        tails, refs = refs[:layers], refs[layers:]
    streams, units, out_buf = refs[:layers], refs[layers], refs[layers + 1]
    core, place = lax.axis_index("chan"), lax.axis_index("tm")
    total = units.shape[1]
    own_rows = pl.ds(pl.multiple_of(core * width, width), width)
    other_rows = pl.ds(pl.multiple_of((1 - core) * width, width), width)

    if earlier:

        @pl.when(lax.axis_index("segment") != stage)
        def _():
            for block, out in zip(earlier, skip_outs):
                out[...] = block[...]

    @pl.when(lax.axis_index("segment") == stage)
    def _():
        for layer in range(layers):
            lag = lags[layer % 4]
            streams[layer][:lag, :] = heads[layer][...] if half else jnp.zeros((lag, depth), jnp.bfloat16)
        if stage == 0:
            rows = inputs[0].shape[0]
            per_half = plan.count // 2
            for side, blocks in ((own_rows, inputs[: n_in // 2]), (other_rows, inputs[n_in // 2 :])):
                for turn, block in enumerate(blocks):
                    t = plan.from_chip(place, turn)

                    @pl.when(t // per_half == half)
                    def _(t=t, block=block, side=side):
                        at = pl.multiple_of(lags[0] + (t - half * per_half) * rows, 16)
                        streams[0][pl.ds(at, rows), side] = block[...]
        else:
            part = inputs[0].shape[0]
            for piece, block in enumerate(inputs[1:]):
                size = block.shape[0]
                at = pl.multiple_of(lags[0] + (1 - core) * part + piece * size, 16)
                streams[0][pl.ds(at, size), :] = block[...]
            streams[0][pl.ds(pl.multiple_of(lags[0] + core * part, 16), part), :] = inputs[0][...]

        for layer in range(layers):
            lag = lags[layer % 4]
            now_buf = streams[layer]
            next_buf, next_lag = (streams[layer + 1], lags[(layer + 1) % 4]) if layer + 1 < layers else (out_buf, 0)
            res = None
            if not (last and layer + 1 == layers):
                res = jnp.concatenate([res_ref[layer, own_rows, :], res_ref[layer, other_rows, :]], 0)

            def tile(row, layer=layer, lag=lag, now_buf=now_buf, next_buf=next_buf, next_lag=next_lag, res=res):
                past = now_buf[pl.ds(row, ROW_TILE), :]
                now = now_buf[pl.ds(lag + row, ROW_TILE), :]
                parts = []
                for conv, bias in ((own_conv, own_bias), (other_conv, other_bias)):
                    shift = jnp.concatenate([bias[layer, 0:1, :], bias[layer, 1:2, :]], 1).astype(jnp.float32)
                    pre = jnp.dot(past, conv[layer, :depth], preferred_element_type=jnp.float32)
                    pre += jnp.dot(now, conv[layer, depth:], preferred_element_type=jnp.float32)
                    pre += shift
                    gate = 0.5 * jnp.tanh(0.5 * pre[:, width:]) + 0.5
                    parts.append((jnp.tanh(pre[:, :width]) * gate).astype(jnp.bfloat16))
                unit = jnp.concatenate(parts, 1)
                units[layer, pl.ds(row, ROW_TILE), :] = unit
                if res is not None:
                    update = jnp.dot(unit, res, preferred_element_type=jnp.float32)
                    next_buf[pl.ds(next_lag + row, ROW_TILE), :] = (now.astype(jnp.float32) + update).astype(jnp.bfloat16)

            steps = total // ROW_TILE
            if steps <= 4:
                for step in range(steps):
                    tile(step * ROW_TILE)
            else:
                pl.loop(0, steps)(lambda step: tile(pl.multiple_of(step * ROW_TILE, ROW_TILE)))

        if not last:
            part = total // 2
            stream_out[...] = out_buf[pl.ds(pl.multiple_of(core * part, 16), part), :]
        if not half:
            for layer in range(layers):
                tails[layer][...] = streams[layer][pl.ds(total, lags[layer % 4]), :]
        for index, out in enumerate(skip_outs):
            rows = out.shape[0]
            t = plan.time_block(place, core, half, index) - half * (plan.count // 2)
            at = pl.multiple_of(jnp.clip(t, 0, total // rows - 1) * rows, rows)
            acc = jnp.zeros((rows, depth), jnp.float32)
            for layer in range(layers):
                unit = units[layer, pl.ds(at, rows), :]
                skip = jnp.concatenate(
                    [
                        jnp.concatenate([part[layer, own_rows, :], part[layer, other_rows, :]], 0)
                        for part in (own_skip, other_skip)
                    ],
                    1,
                )
                acc += jnp.dot(unit, skip, preferred_element_type=jnp.float32)
            out[:, own_rows] = acc[:, :width].astype(out.dtype)
            out[:, other_rows] = acc[:, width:].astype(out.dtype)


def run_section(stage, half, plan, lags, weights, inputs, heads, earlier, rows):
    res_weight = weights[4]
    layers, depth = res_weight.shape[:2]
    total = rows * plan.count // 2
    last = stage == plan.sections - 1
    outs = [jax.ShapeDtypeStruct((rows, depth), jnp.bfloat16)] * plan.blocks
    if not last:
        outs.append(jax.ShapeDtypeStruct((total // 2, depth), jnp.bfloat16))
    if not half:
        outs += [jax.ShapeDtypeStruct((lags[layer % 4], depth), jnp.bfloat16) for layer in range(layers)]
    scratch = [pltpu.VMEM((lags[layer % 4] + total, depth), jnp.bfloat16) for layer in range(layers)]
    scratch += [pltpu.VMEM((layers, total, depth), jnp.bfloat16), pltpu.VMEM((total, depth), jnp.bfloat16)]
    held = 2 * depth * (sum(lags) * 3 + 13 * total)
    got = pl.pallas_call(
        functools.partial(section_kernel, stage, half, plan, lags, len(inputs), len(earlier), last),
        out_shape=outs,
        in_specs=[VMEM] * (len(weights) + len(inputs) + len(heads) + len(earlier)),
        out_specs=[VMEM] * len(outs),
        scratch_shapes=scratch,
        compiler_params=pltpu.CompilerParams(vmem_limit_bytes=held + (12 << 20)),
        cost_estimate=pl.CostEstimate(flops=1, bytes_accessed=1, transcendentals=0),
    )(*weights, *inputs, *heads, *earlier)
    blocks, got = got[: plan.blocks], got[plan.blocks :]
    stream = None
    if not last:
        stream, got = got[0], got[1:]
    return blocks, stream, got


def shards(records, conv_weight, conv_bias, res_weight, skip_weight):
    record_count, rows, width = records.shape
    layers, taps = conv_weight.shape[:2]
    count, sections = lax.axis_size("tm"), lax.axis_size("segment")
    place, segment, core = lax.axis_index("tm"), lax.axis_index("segment"), lax.axis_index("chan")
    lags = [rows // 8, rows, rows * max(1, count // 8), rows * max(1, count // 2)]
    plan = Plan(count, sections, record_count)

    blocks = [
        lax.dynamic_index_in_dim(records, plan.record_at(lax.rem(place + turn, count)), 0, keepdims=False)
        for turn in range(count)
    ]
    blocks, conv_weight = lax.optimization_barrier((blocks, conv_weight))
    for turn in range(1, count):
        blocks[turn] = lax.ppermute(blocks[turn], "tm", [(i, (i + turn) % count) for i in range(count)])
    conv = conv_weight.reshape(layers, taps, 2 * width)
    weights = (conv, swap_cores(conv), conv_bias, swap_cores(conv_bias), res_weight, skip_weight, swap_cores(skip_weight))
    inputs = blocks + [swap_cores(block) for block in blocks]

    skips = {}
    fed = [inputs, inputs]
    for stage in range(sections):
        heads, crossed = (), []
        for half in range(2):
            earlier = []
            if stage == sections - 1:
                for index in range(plan.blocks):
                    members = plan.leave_groups(half, index)[0][1][1:]
                    if members:
                        block = skips[members[0]][index]
                        for member in members[1:]:
                            block = jnp.where(segment == member[0], skips[member][index], block)
                        earlier.append(block)
                earlier = earlier if len(earlier) == plan.blocks else []
            came = fed[half]
            if stage:
                if half:
                    came, heads = lax.optimization_barrier((came, heads))
                else:
                    came, stream = lax.optimization_barrier((came, stream))
                size = came.shape[0] // PIECES
                came = [came] + [swap_cores(came[i * size : (i + 1) * size]) for i in range(PIECES)]
            skips[stage, half], stream, carried = run_section(
                stage, half, plan, lags, weights, came, heads, earlier, rows
            )
            heads = carried
            if stage < sections - 1:
                moved = lax.ppermute(stream, "segment", [(i, (i + 1) % sections) for i in range(sections)])
                crossed.append(moved)
        fed = crossed

    arrived, holds = [], []
    spot = (place * sections + segment) * 2 + core

    def number(device):
        return (device[0] * sections + device[1]) * 2 + device[2]

    for phase in range(2):
        for index in range(plan.blocks):
            for sends, members in plan.leave_groups(phase, index):
                payload = skips[members[0]][index]
                if members[0][0] != sections - 1:
                    for member in members[1:]:
                        payload = jnp.where(segment == member[0], skips[member][index], payload)
                pairs = complete(sends, (count, sections, 2))
                arrived.append(
                    lax.ppermute(
                        payload, ("tm", "segment", "chan"), sorted((number(a), number(b)) for a, b in pairs.items())
                    )
                )
                valid = jnp.bool_(True)
                if len(sends) < 2 * count * sections:
                    valid = functools.reduce(jnp.logical_or, [spot == number(d) for d in sends.values()])
                holds.append(valid.astype(jnp.int32))
    kept, given = pl.pallas_call(
        functools.partial(sum_kernel, len(arrived)),
        out_shape=[jax.ShapeDtypeStruct((rows, width), jnp.bfloat16)] * 2,
        in_specs=[pl.BlockSpec(memory_space=pltpu.SMEM)] + [VMEM] * len(arrived),
        out_specs=[VMEM] * 2,
        compiler_params=pltpu.CompilerParams(vmem_limit_bytes=4 << 20),
    )(jnp.stack(holds), *arrived)
    return pl.pallas_call(
        functools.partial(place_kernel, plan),
        out_shape=jax.ShapeDtypeStruct((plan.share, rows, width), jnp.bfloat16),
        in_specs=[VMEM] * 2,
        out_specs=VMEM,
        compiler_params=pltpu.CompilerParams(vmem_limit_bytes=4 << 20),
    )(kept, swap_cores(given))


def sum_kernel(count, holds, *refs):
    arrived, (kept, given) = refs[:count], refs[count:]
    width = kept.shape[1]
    core = lax.axis_index("chan")
    for side, out in ((core, kept), (1 - core, given)):
        lanes = pl.ds(pl.multiple_of(side * width, width), width)
        total = jnp.zeros(out.shape, jnp.float32)
        for index, block in enumerate(arrived):
            total += jnp.where(holds[index] == 1, block[:, lanes].astype(jnp.float32), 0.0)
        out[...] = total.astype(out.dtype)


def place_kernel(plan, kept, given, out):
    half = lax.axis_index("tm") // (plan.count // 2)
    mine = lax.rem(lax.axis_index("chan") + half + lax.axis_index("segment") + 1, 2)
    for slot in range(plan.share):
        out[slot] = jnp.where(mine == slot, kept[...], given[...])


def solution(mesh):
    return jax.shard_map(
        shards,
        mesh=mesh,
        in_specs=(
            P("groups", "tm", "chan"),
            P("segment", None, None, "chan"),
            P("segment", None, "chan"),
            P("segment", None, None),
            P("segment", None, "chan"),
        ),
        out_specs=P(("groups", "segment"), "tm", "chan"),
        check_vma=False,
    )
```

```python
import functools

import jax
import jax.numpy as jnp
from jax import lax
from jax.experimental import pallas as pl
from jax.experimental.pallas import tpu as pltpu
from jax.sharding import PartitionSpec as P

VMEM = pl.BlockSpec(memory_space=pltpu.VMEM)
ROW_TILE = 512
PIECES = 2


class Plan:
    def __init__(self, count, sections, records):
        self.count, self.sections, self.records = count, sections, records
        self.share = records // sections
        self.whole_group = records <= count // 2
        self.blocks = records // 2 if self.whole_group else max(1, records // 4)

    def owner(self, z):
        return z % self.records % self.sections

    def slot(self, z):
        return z % self.records // self.sections

    def record_at(self, z):
        return self.owner(z) * self.share + self.slot(z)

    def time_block(self, z, core, half, index):
        if self.whole_group:
            return z // self.records * self.records + 2 * index + core
        return half * (self.count // 2) + 2 * index + core

    def landing_core(self, segment, half, slot):
        return (slot + half + segment + 1) % 2

    def from_chip(self, z, turn):
        return lax.rem(z - turn + self.count, self.count)

    def leave_groups(self, phase, index):
        groups = []
        for stage in reversed(range(self.sections)):
            half = phase if stage == self.sections - 1 else 1 - phase
            sends = self.transfers(stage, half, index)
            for known, members in groups:
                if not set(known.values()) & set(sends.values()):
                    known.update(sends)
                    members.append((stage, half))
                    break
            else:
                groups.append((sends, [(stage, half)]))
        return groups

    def transfers(self, stage, half, index):
        sends = {}
        for z in range(self.count):
            for core in range(2):
                t = self.time_block(z, core, half, index)
                if t // (self.count // 2) == half:
                    to = self.owner(z)
                    sends[z, stage, core] = (t, to, self.landing_core(to, half, self.slot(z)))
        return sends


def complete(sends, shape):
    devices = [(z, s, c) for z in range(shape[0]) for s in range(shape[1]) for c in range(shape[2])]
    taken = set(sends.values())
    sources = [d for d in devices if d not in sends]
    targets = [d for d in devices if d not in taken]
    pairs = dict(sends)

    def near(pair):
        a, b = pair
        return (a == b, abs(a[0] - b[0]), a[1] != b[1])

    for source in sources:
        target = min(targets, key=lambda b: near((source, b)))
        targets.remove(target)
        pairs[source] = target
    for a in [d for d in sources if pairs[d] == d]:
        b = next((d for d in sources if d != a and pairs[d] != a), None)
        if b is not None:
            pairs[a], pairs[b] = pairs[b], pairs[a]
    return pairs


def swap_cores(block):
    return lax.ppermute(block, "chan", [(0, 1), (1, 0)])


def section_kernel(stage, half, plan, lags, n_in, n_earlier, last, *refs):
    own_conv, other_conv, own_bias, other_bias, res_ref, own_skip, other_skip = refs[:7]
    inputs, refs = refs[7 : 7 + n_in], refs[7 + n_in :]
    layers, depth = res_ref.shape[:2]
    width = depth // 2
    heads = ()
    if half:
        heads, refs = refs[:layers], refs[layers:]
    earlier, refs = refs[:n_earlier], refs[n_earlier:]
    skip_outs, refs = refs[: plan.blocks], refs[plan.blocks :]
    if not last:
        stream_out, refs = refs[0], refs[1:]
    if not half:
        tails, refs = refs[:layers], refs[layers:]
    streams, units, out_buf = refs[:layers], refs[layers], refs[layers + 1]
    core, place = lax.axis_index("chan"), lax.axis_index("tm")
    total = units.shape[1]
    own_rows = pl.ds(pl.multiple_of(core * width, width), width)
    other_rows = pl.ds(pl.multiple_of((1 - core) * width, width), width)

    if earlier:

        @pl.when(lax.axis_index("segment") != stage)
        def _():
            for block, out in zip(earlier, skip_outs):
                out[...] = block[...]

    @pl.when(lax.axis_index("segment") == stage)
    def _():
        for layer in range(layers):
            lag = lags[layer % 4]
            streams[layer][:lag, :] = heads[layer][...] if half else jnp.zeros((lag, depth), jnp.bfloat16)
        if stage == 0:
            rows = inputs[0].shape[0]
            per_half = plan.count // 2
            for side, blocks in ((own_rows, inputs[: n_in // 2]), (other_rows, inputs[n_in // 2 :])):
                for turn, block in enumerate(blocks):
                    t = plan.from_chip(place, turn)

                    @pl.when(t // per_half == half)
                    def _(t=t, block=block, side=side):
                        at = pl.multiple_of(lags[0] + (t - half * per_half) * rows, 16)
                        streams[0][pl.ds(at, rows), side] = block[...]
        else:
            part = inputs[0].shape[0]
            for piece, block in enumerate(inputs[1:]):
                size = block.shape[0]
                at = pl.multiple_of(lags[0] + (1 - core) * part + piece * size, 16)
                streams[0][pl.ds(at, size), :] = block[...]
            streams[0][pl.ds(pl.multiple_of(lags[0] + core * part, 16), part), :] = inputs[0][...]

        for layer in range(layers):
            lag = lags[layer % 4]
            now_buf = streams[layer]
            next_buf, next_lag = (streams[layer + 1], lags[(layer + 1) % 4]) if layer + 1 < layers else (out_buf, 0)
            res = None
            if not (last and layer + 1 == layers):
                res = jnp.concatenate([res_ref[layer, own_rows, :], res_ref[layer, other_rows, :]], 0)

            def tile(row, layer=layer, lag=lag, now_buf=now_buf, next_buf=next_buf, next_lag=next_lag, res=res):
                past = now_buf[pl.ds(row, ROW_TILE), :]
                now = now_buf[pl.ds(lag + row, ROW_TILE), :]
                parts = []
                both = jnp.concatenate([past, now], 1)
                for conv, bias in ((own_conv, own_bias), (other_conv, other_bias)):
                    shift = jnp.concatenate([bias[layer, 0:1, :], bias[layer, 1:2, :]], 1).astype(jnp.float32)
                    pre = jnp.dot(both, conv[layer], preferred_element_type=jnp.float32)
                    pre += shift
                    gate = 0.5 * jnp.tanh(0.5 * pre[:, width:]) + 0.5
                    parts.append((jnp.tanh(pre[:, :width]) * gate).astype(jnp.bfloat16))
                unit = jnp.concatenate(parts, 1)
                units[layer, pl.ds(row, ROW_TILE), :] = unit
                if res is not None:
                    update = jnp.dot(unit, res, preferred_element_type=jnp.float32)
                    next_buf[pl.ds(next_lag + row, ROW_TILE), :] = (now.astype(jnp.float32) + update).astype(jnp.bfloat16)

            steps = total // ROW_TILE
            if steps <= 4:
                for step in range(steps):
                    tile(step * ROW_TILE)
            else:
                pl.loop(0, steps)(lambda step: tile(pl.multiple_of(step * ROW_TILE, ROW_TILE)))

        if not last:
            part = total // 2
            stream_out[...] = out_buf[pl.ds(pl.multiple_of(core * part, 16), part), :]
        if not half:
            for layer in range(layers):
                tails[layer][...] = streams[layer][pl.ds(total, lags[layer % 4]), :]
        for index, out in enumerate(skip_outs):
            rows = out.shape[0]
            t = plan.time_block(place, core, half, index) - half * (plan.count // 2)
            at = pl.multiple_of(jnp.clip(t, 0, total // rows - 1) * rows, rows)
            acc = jnp.zeros((rows, depth), jnp.float32)
            for layer in range(layers):
                unit = units[layer, pl.ds(at, rows), :]
                skip = jnp.concatenate(
                    [
                        jnp.concatenate([part[layer, own_rows, :], part[layer, other_rows, :]], 0)
                        for part in (own_skip, other_skip)
                    ],
                    1,
                )
                acc += jnp.dot(unit, skip, preferred_element_type=jnp.float32)
            out[:, own_rows] = acc[:, :width].astype(out.dtype)
            out[:, other_rows] = acc[:, width:].astype(out.dtype)


def run_section(stage, half, plan, lags, weights, inputs, heads, earlier, rows):
    res_weight = weights[4]
    layers, depth = res_weight.shape[:2]
    total = rows * plan.count // 2
    last = stage == plan.sections - 1
    outs = [jax.ShapeDtypeStruct((rows, depth), jnp.bfloat16)] * plan.blocks
    if not last:
        outs.append(jax.ShapeDtypeStruct((total // 2, depth), jnp.bfloat16))
    if not half:
        outs += [jax.ShapeDtypeStruct((lags[layer % 4], depth), jnp.bfloat16) for layer in range(layers)]
    scratch = [pltpu.VMEM((lags[layer % 4] + total, depth), jnp.bfloat16) for layer in range(layers)]
    scratch += [pltpu.VMEM((layers, total, depth), jnp.bfloat16), pltpu.VMEM((total, depth), jnp.bfloat16)]
    held = 2 * depth * (sum(lags) * 3 + 13 * total)
    got = pl.pallas_call(
        functools.partial(section_kernel, stage, half, plan, lags, len(inputs), len(earlier), last),
        out_shape=outs,
        in_specs=[VMEM] * (len(weights) + len(inputs) + len(heads) + len(earlier)),
        out_specs=[VMEM] * len(outs),
        scratch_shapes=scratch,
        compiler_params=pltpu.CompilerParams(vmem_limit_bytes=held + (12 << 20)),
        cost_estimate=pl.CostEstimate(flops=1, bytes_accessed=1, transcendentals=0),
    )(*weights, *inputs, *heads, *earlier)
    blocks, got = got[: plan.blocks], got[plan.blocks :]
    stream = None
    if not last:
        stream, got = got[0], got[1:]
    return blocks, stream, got


def shards(records, conv_weight, conv_bias, res_weight, skip_weight):
    record_count, rows, width = records.shape
    layers, taps = conv_weight.shape[:2]
    count, sections = lax.axis_size("tm"), lax.axis_size("segment")
    place, segment, core = lax.axis_index("tm"), lax.axis_index("segment"), lax.axis_index("chan")
    lags = [rows // 8, rows, rows * max(1, count // 8), rows * max(1, count // 2)]
    plan = Plan(count, sections, record_count)

    blocks = [
        lax.dynamic_index_in_dim(records, plan.record_at(lax.rem(place + turn, count)), 0, keepdims=False)
        for turn in range(count)
    ]
    for turn in range(1, count):
        blocks[turn] = lax.ppermute(blocks[turn], "tm", [(i, (i + turn) % count) for i in range(count)])
    conv = conv_weight.reshape(layers, taps, 2 * width)
    weights = (conv, swap_cores(conv), conv_bias, swap_cores(conv_bias), res_weight, skip_weight, swap_cores(skip_weight))
    inputs = blocks + [swap_cores(block) for block in blocks]

    skips = {}
    fed = [inputs, inputs]
    for stage in range(sections):
        heads, crossed = (), []
        for half in range(2):
            earlier = []
            if stage == sections - 1:
                for index in range(plan.blocks):
                    members = plan.leave_groups(half, index)[0][1][1:]
                    if members:
                        block = skips[members[0]][index]
                        for member in members[1:]:
                            block = jnp.where(segment == member[0], skips[member][index], block)
                        earlier.append(block)
                earlier = earlier if len(earlier) == plan.blocks else []
            came = fed[half]
            if stage:
                if half:
                    came, heads = lax.optimization_barrier((came, heads))
                else:
                    came, stream = lax.optimization_barrier((came, stream))
                size = came.shape[0] // PIECES
                came = [came] + [swap_cores(came[i * size : (i + 1) * size]) for i in range(PIECES)]
            skips[stage, half], stream, carried = run_section(
                stage, half, plan, lags, weights, came, heads, earlier, rows
            )
            heads = carried
            if stage < sections - 1:
                moved = lax.ppermute(stream, "segment", [(i, (i + 1) % sections) for i in range(sections)])
                crossed.append(moved)
        fed = crossed

    arrived, holds = [], []
    spot = (place * sections + segment) * 2 + core

    def number(device):
        return (device[0] * sections + device[1]) * 2 + device[2]

    for phase in range(2):
        for index in range(plan.blocks):
            for sends, members in plan.leave_groups(phase, index):
                payload = skips[members[0]][index]
                if members[0][0] != sections - 1:
                    for member in members[1:]:
                        payload = jnp.where(segment == member[0], skips[member][index], payload)
                pairs = complete(sends, (count, sections, 2))
                arrived.append(
                    lax.ppermute(
                        payload, ("tm", "segment", "chan"), sorted((number(a), number(b)) for a, b in pairs.items())
                    )
                )
                valid = jnp.bool_(True)
                if len(sends) < 2 * count * sections:
                    valid = functools.reduce(jnp.logical_or, [spot == number(d) for d in sends.values()])
                holds.append(valid.astype(jnp.int32))
    kept, given = pl.pallas_call(
        functools.partial(sum_kernel, len(arrived)),
        out_shape=[jax.ShapeDtypeStruct((rows, width), jnp.bfloat16)] * 2,
        in_specs=[pl.BlockSpec(memory_space=pltpu.SMEM)] + [VMEM] * len(arrived),
        out_specs=[VMEM] * 2,
        compiler_params=pltpu.CompilerParams(vmem_limit_bytes=4 << 20),
    )(jnp.stack(holds), *arrived)
    return pl.pallas_call(
        functools.partial(place_kernel, plan),
        out_shape=jax.ShapeDtypeStruct((plan.share, rows, width), jnp.bfloat16),
        in_specs=[VMEM] * 2,
        out_specs=VMEM,
        compiler_params=pltpu.CompilerParams(vmem_limit_bytes=4 << 20),
    )(kept, swap_cores(given))


def sum_kernel(count, holds, *refs):
    arrived, (kept, given) = refs[:count], refs[count:]
    width = kept.shape[1]
    core = lax.axis_index("chan")
    for side, out in ((core, kept), (1 - core, given)):
        lanes = pl.ds(pl.multiple_of(side * width, width), width)
        total = jnp.zeros(out.shape, jnp.float32)
        for index, block in enumerate(arrived):
            total += jnp.where(holds[index] == 1, block[:, lanes].astype(jnp.float32), 0.0)
        out[...] = total.astype(out.dtype)


def place_kernel(plan, kept, given, out):
    half = lax.axis_index("tm") // (plan.count // 2)
    mine = lax.rem(lax.axis_index("chan") + half + lax.axis_index("segment") + 1, 2)
    for slot in range(plan.share):
        out[slot] = jnp.where(mine == slot, kept[...], given[...])


def solution(mesh):
    return jax.shard_map(
        shards,
        mesh=mesh,
        in_specs=(
            P("groups", "tm", "chan"),
            P("segment", None, None, "chan"),
            P("segment", None, "chan"),
            P("segment", None, None),
            P("segment", None, "chan"),
        ),
        out_specs=P(("groups", "segment"), "tm", "chan"),
        check_vma=False,
    )
```

```python
import functools

import jax
import jax.numpy as jnp
from jax import lax
from jax.experimental import pallas as pl
from jax.experimental.pallas import tpu as pltpu
from jax.sharding import PartitionSpec as P

VMEM = pl.BlockSpec(memory_space=pltpu.VMEM)
ROW_TILE = 512
PIECES = 2


class Plan:
    def __init__(self, count, sections, records):
        self.count, self.sections, self.records = count, sections, records
        self.share = records // sections
        self.whole_group = records <= count // 2
        self.blocks = records // 2 if self.whole_group else max(1, records // 4)

    def owner(self, z):
        return z % self.records % self.sections

    def slot(self, z):
        return z % self.records // self.sections

    def record_at(self, z):
        return self.owner(z) * self.share + self.slot(z)

    def time_block(self, z, core, half, index):
        if self.whole_group:
            return z // self.records * self.records + 2 * index + core
        return half * (self.count // 2) + 2 * index + core

    def landing_core(self, segment, half, slot):
        return (slot + half + segment + 1) % 2

    def from_chip(self, z, turn):
        return lax.rem(z - turn + self.count, self.count)

    def leave_groups(self, phase, index):
        groups = []
        for stage in reversed(range(self.sections)):
            half = phase if stage == self.sections - 1 else 1 - phase
            sends = self.transfers(stage, half, index)
            for known, members in groups:
                if not set(known.values()) & set(sends.values()):
                    known.update(sends)
                    members.append((stage, half))
                    break
            else:
                groups.append((sends, [(stage, half)]))
        return groups

    def transfers(self, stage, half, index):
        sends = {}
        for z in range(self.count):
            for core in range(2):
                t = self.time_block(z, core, half, index)
                if t // (self.count // 2) == half:
                    to = self.owner(z)
                    sends[z, stage, core] = (t, to, self.landing_core(to, half, self.slot(z)))
        return sends


def complete(sends, shape):
    devices = [(z, s, c) for z in range(shape[0]) for s in range(shape[1]) for c in range(shape[2])]
    taken = set(sends.values())
    sources = [d for d in devices if d not in sends]
    targets = [d for d in devices if d not in taken]
    pairs = dict(sends)

    def near(pair):
        a, b = pair
        return (a == b, abs(a[0] - b[0]), a[1] != b[1])

    for source in sources:
        target = min(targets, key=lambda b: near((source, b)))
        targets.remove(target)
        pairs[source] = target
    for a in [d for d in sources if pairs[d] == d]:
        b = next((d for d in sources if d != a and pairs[d] != a), None)
        if b is not None:
            pairs[a], pairs[b] = pairs[b], pairs[a]
    return pairs


def swap_cores(block):
    return lax.ppermute(block, "chan", [(0, 1), (1, 0)])


def section_kernel(stage, half, plan, lags, n_in, n_earlier, last, *refs):
    own_conv, other_conv, own_bias, other_bias, res_ref, own_skip, other_skip = refs[:7]
    inputs, refs = refs[7 : 7 + n_in], refs[7 + n_in :]
    layers, depth = res_ref.shape[:2]
    width = depth // 2
    heads = ()
    if half:
        heads, refs = refs[:layers], refs[layers:]
    earlier, refs = refs[:n_earlier], refs[n_earlier:]
    skip_outs, refs = refs[: plan.blocks], refs[plan.blocks :]
    if not last:
        stream_out, refs = refs[0], refs[1:]
    if not half:
        tails, refs = refs[:layers], refs[layers:]
    streams, units, out_buf = refs[:layers], refs[layers], refs[layers + 1]
    core, place = lax.axis_index("chan"), lax.axis_index("tm")
    total = units.shape[1]
    own_rows = pl.ds(pl.multiple_of(core * width, width), width)
    other_rows = pl.ds(pl.multiple_of((1 - core) * width, width), width)

    if earlier:

        @pl.when(lax.axis_index("segment") != stage)
        def _():
            for block, out in zip(earlier, skip_outs):
                out[...] = block[...]

    @pl.when(lax.axis_index("segment") == stage)
    def _():
        for layer in range(layers):
            lag = lags[layer % 4]
            streams[layer][:lag, :] = heads[layer][...] if half else jnp.zeros((lag, depth), jnp.bfloat16)
        if stage == 0:
            rows = inputs[0].shape[0]
            per_half = plan.count // 2
            for side, blocks in ((own_rows, inputs[: n_in // 2]), (other_rows, inputs[n_in // 2 :])):
                for turn, block in enumerate(blocks):
                    t = plan.from_chip(place, turn)

                    @pl.when(t // per_half == half)
                    def _(t=t, block=block, side=side):
                        at = pl.multiple_of(lags[0] + (t - half * per_half) * rows, 16)
                        streams[0][pl.ds(at, rows), side] = block[...]
        else:
            part = inputs[0].shape[0]
            for piece, block in enumerate(inputs[1:]):
                size = block.shape[0]
                at = pl.multiple_of(lags[0] + (1 - core) * part + piece * size, 16)
                streams[0][pl.ds(at, size), :] = block[...]
            streams[0][pl.ds(pl.multiple_of(lags[0] + core * part, 16), part), :] = inputs[0][...]

        for layer in range(layers):
            lag = lags[layer % 4]
            now_buf = streams[layer]
            next_buf, next_lag = (streams[layer + 1], lags[(layer + 1) % 4]) if layer + 1 < layers else (out_buf, 0)
            res = None
            if not (last and layer + 1 == layers):
                res = jnp.concatenate([res_ref[layer, own_rows, :], res_ref[layer, other_rows, :]], 0)

            def tile(row, layer=layer, lag=lag, now_buf=now_buf, next_buf=next_buf, next_lag=next_lag, res=res):
                past = now_buf[pl.ds(row, ROW_TILE), :]
                now = now_buf[pl.ds(lag + row, ROW_TILE), :]
                parts = []
                both = jnp.concatenate([past, now], 1)
                for conv, bias in ((own_conv, own_bias), (other_conv, other_bias)):
                    shift = jnp.concatenate([bias[layer, 0:1, :], bias[layer, 1:2, :]], 1).astype(jnp.float32)
                    pre = jnp.dot(both, conv[layer], preferred_element_type=jnp.float32)
                    pre += shift
                    gate = 0.5 * jnp.tanh(0.5 * pre[:, width:]) + 0.5
                    parts.append((jnp.tanh(pre[:, :width]) * gate).astype(jnp.bfloat16))
                unit = jnp.concatenate(parts, 1)
                units[layer, pl.ds(row, ROW_TILE), :] = unit
                if res is not None:
                    update = jnp.dot(unit, res, preferred_element_type=jnp.float32)
                    next_buf[pl.ds(next_lag + row, ROW_TILE), :] = (now.astype(jnp.float32) + update).astype(jnp.bfloat16)

            steps = total // ROW_TILE
            if steps <= 4:
                for step in range(steps):
                    tile(step * ROW_TILE)
            else:
                pl.loop(0, steps)(lambda step: tile(pl.multiple_of(step * ROW_TILE, ROW_TILE)))

        if not last:
            part = total // 2
            stream_out[...] = out_buf[pl.ds(pl.multiple_of(core * part, 16), part), :]
        if not half:
            for layer in range(layers):
                tails[layer][...] = streams[layer][pl.ds(total, lags[layer % 4]), :]
        for index, out in enumerate(skip_outs):
            rows = out.shape[0]
            t = plan.time_block(place, core, half, index) - half * (plan.count // 2)
            at = pl.multiple_of(jnp.clip(t, 0, total // rows - 1) * rows, rows)
            acc = jnp.zeros((rows, depth), jnp.float32)
            for layer in range(layers):
                unit = units[layer, pl.ds(at, rows), :]
                skip = jnp.concatenate(
                    [
                        jnp.concatenate([part[layer, own_rows, :], part[layer, other_rows, :]], 0)
                        for part in (own_skip, other_skip)
                    ],
                    1,
                )
                acc += jnp.dot(unit, skip, preferred_element_type=jnp.float32)
            out[:, own_rows] = acc[:, :width].astype(out.dtype)
            out[:, other_rows] = acc[:, width:].astype(out.dtype)


def run_section(stage, half, plan, lags, weights, inputs, heads, earlier, rows):
    res_weight = weights[4]
    layers, depth = res_weight.shape[:2]
    total = rows * plan.count // 2
    last = stage == plan.sections - 1
    outs = [jax.ShapeDtypeStruct((rows, depth), jnp.bfloat16)] * plan.blocks
    if not last:
        outs.append(jax.ShapeDtypeStruct((total // 2, depth), jnp.bfloat16))
    if not half:
        outs += [jax.ShapeDtypeStruct((lags[layer % 4], depth), jnp.bfloat16) for layer in range(layers)]
    scratch = [pltpu.VMEM((lags[layer % 4] + total, depth), jnp.bfloat16) for layer in range(layers)]
    scratch += [pltpu.VMEM((layers, total, depth), jnp.bfloat16), pltpu.VMEM((total, depth), jnp.bfloat16)]
    held = 2 * depth * (sum(lags) * 3 + 13 * total)
    got = pl.pallas_call(
        functools.partial(section_kernel, stage, half, plan, lags, len(inputs), len(earlier), last),
        out_shape=outs,
        in_specs=[VMEM] * (len(weights) + len(inputs) + len(heads) + len(earlier)),
        out_specs=[VMEM] * len(outs),
        scratch_shapes=scratch,
        compiler_params=pltpu.CompilerParams(vmem_limit_bytes=held + (12 << 20)),
        cost_estimate=pl.CostEstimate(flops=1, bytes_accessed=1, transcendentals=0),
    )(*weights, *inputs, *heads, *earlier)
    blocks, got = got[: plan.blocks], got[plan.blocks :]
    stream = None
    if not last:
        stream, got = got[0], got[1:]
    return blocks, stream, got


def shards(records, conv_weight, conv_bias, res_weight, skip_weight):
    record_count, rows, width = records.shape
    layers, taps = conv_weight.shape[:2]
    count, sections = lax.axis_size("tm"), lax.axis_size("segment")
    place, segment, core = lax.axis_index("tm"), lax.axis_index("segment"), lax.axis_index("chan")
    lags = [rows // 8, rows, rows * max(1, count // 8), rows * max(1, count // 2)]
    plan = Plan(count, sections, record_count)

    blocks = [
        lax.dynamic_index_in_dim(records, plan.record_at(lax.rem(place + turn, count)), 0, keepdims=False)
        for turn in range(count)
    ]
    for turn in range(1, count):
        blocks[turn] = lax.ppermute(blocks[turn], "tm", [(i, (i + turn) % count) for i in range(count)])
    conv = conv_weight.reshape(layers, taps, 2 * width)
    other_conv = swap_cores(conv_weight).reshape(layers, taps, 2 * width)
    weights = (conv, other_conv, conv_bias, swap_cores(conv_bias), res_weight, skip_weight, swap_cores(skip_weight))
    blocks[1], conv, other_conv = lax.optimization_barrier((blocks[1], conv, other_conv))
    weights = (conv, other_conv, *weights[2:])
    order = list(range(1, count))
    for before, turn in zip(order, order[1:]):
        blocks[turn] = lax.optimization_barrier((blocks[turn], blocks[before]))[0]
    inputs = blocks + [swap_cores(block) for block in blocks]

    skips = {}
    fed = [inputs, inputs]
    for stage in range(sections):
        heads, crossed = (), []
        for half in range(2):
            earlier = []
            if stage == sections - 1:
                for index in range(plan.blocks):
                    members = plan.leave_groups(half, index)[0][1][1:]
                    if members:
                        block = skips[members[0]][index]
                        for member in members[1:]:
                            block = jnp.where(segment == member[0], skips[member][index], block)
                        earlier.append(block)
                earlier = earlier if len(earlier) == plan.blocks else []
            came = fed[half]
            if stage:
                if half:
                    came, heads = lax.optimization_barrier((came, heads))
                else:
                    came, stream = lax.optimization_barrier((came, stream))
                size = came.shape[0] // PIECES
                came = [came] + [swap_cores(came[i * size : (i + 1) * size]) for i in range(PIECES)]
            skips[stage, half], stream, carried = run_section(
                stage, half, plan, lags, weights, came, heads, earlier, rows
            )
            heads = carried
            if stage < sections - 1:
                moved = lax.ppermute(stream, "segment", [(i, (i + 1) % sections) for i in range(sections)])
                crossed.append(moved)
        fed = crossed

    arrived, holds = [], []
    spot = (place * sections + segment) * 2 + core

    def number(device):
        return (device[0] * sections + device[1]) * 2 + device[2]

    for phase in range(2):
        for index in range(plan.blocks):
            for sends, members in plan.leave_groups(phase, index):
                payload = skips[members[0]][index]
                if members[0][0] != sections - 1:
                    for member in members[1:]:
                        payload = jnp.where(segment == member[0], skips[member][index], payload)
                pairs = complete(sends, (count, sections, 2))
                arrived.append(
                    lax.ppermute(
                        payload, ("tm", "segment", "chan"), sorted((number(a), number(b)) for a, b in pairs.items())
                    )
                )
                if len(sends) < 2 * count * sections:
                    valid = functools.reduce(jnp.logical_or, [spot == number(d) for d in sends.values()])
                    holds.append(valid.astype(jnp.int32))
                else:
                    holds.append(1)
    masks = [] if all(isinstance(hold, int) for hold in holds) else [jnp.stack(holds)]
    kept, given = pl.pallas_call(
        functools.partial(sum_kernel, len(masks)),
        out_shape=[jax.ShapeDtypeStruct((rows, width), jnp.bfloat16)] * 2,
        in_specs=[pl.BlockSpec(memory_space=pltpu.SMEM)] * len(masks) + [VMEM] * len(arrived),
        out_specs=[VMEM] * 2,
        compiler_params=pltpu.CompilerParams(vmem_limit_bytes=4 << 20),
    )(*masks, *arrived)
    return pl.pallas_call(
        functools.partial(place_kernel, plan),
        out_shape=jax.ShapeDtypeStruct((plan.share, rows, width), jnp.bfloat16),
        in_specs=[VMEM] * 2,
        out_specs=VMEM,
        compiler_params=pltpu.CompilerParams(vmem_limit_bytes=4 << 20),
    )(kept, swap_cores(given))


def sum_kernel(masked, *refs):
    masks, arrived, (kept, given) = refs[:masked], refs[masked:-2], refs[-2:]
    width = kept.shape[1]
    core = lax.axis_index("chan")
    for side, out in ((core, kept), (1 - core, given)):
        lanes = pl.ds(pl.multiple_of(side * width, width), width)
        total = jnp.zeros(out.shape, jnp.float32)
        for index, block in enumerate(arrived):
            part = block[:, lanes].astype(jnp.float32)
            total += jnp.where(masks[0][index] == 1, part, 0.0) if masked else part
        out[...] = total.astype(out.dtype)


def place_kernel(plan, kept, given, out):
    half = lax.axis_index("tm") // (plan.count // 2)
    mine = lax.rem(lax.axis_index("chan") + half + lax.axis_index("segment") + 1, 2)
    for slot in range(plan.share):
        out[slot] = jnp.where(mine == slot, kept[...], given[...])


def solution(mesh):
    return jax.shard_map(
        shards,
        mesh=mesh,
        in_specs=(
            P("groups", "tm", "chan"),
            P("segment", None, None, "chan"),
            P("segment", None, "chan"),
            P("segment", None, None),
            P("segment", None, "chan"),
        ),
        out_specs=P(("groups", "segment"), "tm", "chan"),
        check_vma=False,
    )
```

```python
import functools

import jax
import jax.numpy as jnp
from jax import lax
from jax.experimental import pallas as pl
from jax.experimental.pallas import tpu as pltpu
from jax.sharding import PartitionSpec as P

VMEM = pl.BlockSpec(memory_space=pltpu.VMEM)
ROW_TILE = 512
PIECES = 2


class Plan:
    def __init__(self, count, sections, records):
        self.count, self.sections, self.records = count, sections, records
        self.share = records // sections
        self.whole_group = records <= count // 2
        self.blocks = records // 2 if self.whole_group else max(1, records // 4)

    def owner(self, z):
        return z % self.records % self.sections

    def slot(self, z):
        return z % self.records // self.sections

    def record_at(self, z):
        return self.owner(z) * self.share + self.slot(z)

    def time_block(self, z, core, half, index):
        if self.whole_group:
            return z // self.records * self.records + 2 * index + core
        return half * (self.count // 2) + 2 * index + core

    def landing_core(self, segment, half, slot):
        return (slot + half + segment + 1) % 2

    def from_chip(self, z, turn):
        return lax.rem(z - turn + self.count, self.count)

    def leave_groups(self, phase, index):
        groups = []
        for stage in reversed(range(self.sections)):
            half = phase if stage == self.sections - 1 else 1 - phase
            sends = self.transfers(stage, half, index)
            for known, members in groups:
                if not set(known.values()) & set(sends.values()):
                    known.update(sends)
                    members.append((stage, half))
                    break
            else:
                groups.append((sends, [(stage, half)]))
        return groups

    def transfers(self, stage, half, index):
        sends = {}
        for z in range(self.count):
            for core in range(2):
                t = self.time_block(z, core, half, index)
                if t // (self.count // 2) == half:
                    to = self.owner(z)
                    sends[z, stage, core] = (t, to, self.landing_core(to, half, self.slot(z)))
        return sends


def complete(sends, shape):
    devices = [(z, s, c) for z in range(shape[0]) for s in range(shape[1]) for c in range(shape[2])]
    taken = set(sends.values())
    sources = [d for d in devices if d not in sends]
    targets = [d for d in devices if d not in taken]
    pairs = dict(sends)

    def near(pair):
        a, b = pair
        return (a == b, abs(a[0] - b[0]), a[1] != b[1])

    for source in sources:
        target = min(targets, key=lambda b: near((source, b)))
        targets.remove(target)
        pairs[source] = target
    for a in [d for d in sources if pairs[d] == d]:
        b = next((d for d in sources if d != a and pairs[d] != a), None)
        if b is not None:
            pairs[a], pairs[b] = pairs[b], pairs[a]
    return pairs


def swap_cores(block):
    return lax.ppermute(block, "chan", [(0, 1), (1, 0)])


def section_kernel(stage, half, plan, lags, n_in, n_earlier, last, *refs):
    own_conv, other_conv, own_bias, other_bias, res_ref, own_skip, other_skip = refs[:7]
    inputs, refs = refs[7 : 7 + n_in], refs[7 + n_in :]
    layers, depth = res_ref.shape[:2]
    width = depth // 2
    heads = ()
    if half:
        heads, refs = refs[:layers], refs[layers:]
    earlier, refs = refs[:n_earlier], refs[n_earlier:]
    skip_outs, refs = refs[: plan.blocks], refs[plan.blocks :]
    if not last:
        stream_out, refs = refs[0], refs[1:]
    if not half:
        tails, refs = refs[:layers], refs[layers:]
    streams, units, out_buf = refs[:layers], refs[layers], refs[layers + 1]
    core, place = lax.axis_index("chan"), lax.axis_index("tm")
    total = units.shape[1]
    own_rows = pl.ds(pl.multiple_of(core * width, width), width)
    other_rows = pl.ds(pl.multiple_of((1 - core) * width, width), width)

    if earlier:

        @pl.when(lax.axis_index("segment") != stage)
        def _():
            for block, out in zip(earlier, skip_outs):
                out[...] = block[...]

    @pl.when(lax.axis_index("segment") == stage)
    def _():
        for layer in range(layers):
            lag = lags[layer % 4]
            streams[layer][:lag, :] = heads[layer][...] if half else jnp.zeros((lag, depth), jnp.bfloat16)
        if stage == 0:
            rows = inputs[0].shape[0]
            per_half = plan.count // 2
            for turn in range(plan.count):
                t = plan.from_chip(place, turn)

                @pl.when(t // per_half == half)
                def _(t=t, turn=turn):
                    at = pl.multiple_of(lags[0] + (t - half * per_half) * rows, 16)
                    streams[0][pl.ds(at, rows), own_rows] = inputs[turn][...]
                    streams[0][pl.ds(at, rows), other_rows] = inputs[plan.count][turn * rows : (turn + 1) * rows, :]
        else:
            part = inputs[0].shape[0]
            for piece, block in enumerate(inputs[1:]):
                size = block.shape[0]
                at = pl.multiple_of(lags[0] + (1 - core) * part + piece * size, 16)
                streams[0][pl.ds(at, size), :] = block[...]
            streams[0][pl.ds(pl.multiple_of(lags[0] + core * part, 16), part), :] = inputs[0][...]

        for layer in range(layers):
            lag = lags[layer % 4]
            now_buf = streams[layer]
            next_buf, next_lag = (streams[layer + 1], lags[(layer + 1) % 4]) if layer + 1 < layers else (out_buf, 0)
            res = None
            if not (last and layer + 1 == layers):
                res = jnp.concatenate([res_ref[layer, own_rows, :], res_ref[layer, other_rows, :]], 0)

            def tile(row, layer=layer, lag=lag, now_buf=now_buf, next_buf=next_buf, next_lag=next_lag, res=res):
                past = now_buf[pl.ds(row, ROW_TILE), :]
                now = now_buf[pl.ds(lag + row, ROW_TILE), :]
                parts = []
                both = jnp.concatenate([past, now], 1)
                for conv, bias in ((own_conv, own_bias), (other_conv, other_bias)):
                    shift = jnp.concatenate([bias[layer, 0:1, :], bias[layer, 1:2, :]], 1).astype(jnp.float32)
                    pre = jnp.dot(both, conv[layer], preferred_element_type=jnp.float32)
                    pre += shift
                    gate = 0.5 * jnp.tanh(0.5 * pre[:, width:]) + 0.5
                    parts.append((jnp.tanh(pre[:, :width]) * gate).astype(jnp.bfloat16))
                unit = jnp.concatenate(parts, 1)
                units[layer, pl.ds(row, ROW_TILE), :] = unit
                if res is not None:
                    update = jnp.dot(unit, res, preferred_element_type=jnp.float32)
                    next_buf[pl.ds(next_lag + row, ROW_TILE), :] = (now.astype(jnp.float32) + update).astype(jnp.bfloat16)

            steps = total // ROW_TILE
            if steps <= 4:
                for step in range(steps):
                    tile(step * ROW_TILE)
            else:
                pl.loop(0, steps)(lambda step: tile(pl.multiple_of(step * ROW_TILE, ROW_TILE)))

        if not last:
            part = total // 2
            stream_out[...] = out_buf[pl.ds(pl.multiple_of(core * part, 16), part), :]
        if not half:
            for layer in range(layers):
                tails[layer][...] = streams[layer][pl.ds(total, lags[layer % 4]), :]
        for index, out in enumerate(skip_outs):
            rows = out.shape[0]
            t = plan.time_block(place, core, half, index) - half * (plan.count // 2)
            at = pl.multiple_of(jnp.clip(t, 0, total // rows - 1) * rows, rows)
            acc = jnp.zeros((rows, depth), jnp.float32)
            for layer in range(layers):
                unit = units[layer, pl.ds(at, rows), :]
                skip = jnp.concatenate(
                    [
                        jnp.concatenate([part[layer, own_rows, :], part[layer, other_rows, :]], 0)
                        for part in (own_skip, other_skip)
                    ],
                    1,
                )
                acc += jnp.dot(unit, skip, preferred_element_type=jnp.float32)
            out[:, own_rows] = acc[:, :width].astype(out.dtype)
            out[:, other_rows] = acc[:, width:].astype(out.dtype)


def run_section(stage, half, plan, lags, weights, inputs, heads, earlier, rows):
    res_weight = weights[4]
    layers, depth = res_weight.shape[:2]
    total = rows * plan.count // 2
    last = stage == plan.sections - 1
    outs = [jax.ShapeDtypeStruct((rows, depth), jnp.bfloat16)] * plan.blocks
    if not last:
        outs.append(jax.ShapeDtypeStruct((total // 2, depth), jnp.bfloat16))
    if not half:
        outs += [jax.ShapeDtypeStruct((lags[layer % 4], depth), jnp.bfloat16) for layer in range(layers)]
    scratch = [pltpu.VMEM((lags[layer % 4] + total, depth), jnp.bfloat16) for layer in range(layers)]
    scratch += [pltpu.VMEM((layers, total, depth), jnp.bfloat16), pltpu.VMEM((total, depth), jnp.bfloat16)]
    held = 2 * depth * (sum(lags) * 3 + 13 * total)
    got = pl.pallas_call(
        functools.partial(section_kernel, stage, half, plan, lags, len(inputs), len(earlier), last),
        out_shape=outs,
        in_specs=[VMEM] * (len(weights) + len(inputs) + len(heads) + len(earlier)),
        out_specs=[VMEM] * len(outs),
        scratch_shapes=scratch,
        compiler_params=pltpu.CompilerParams(vmem_limit_bytes=held + (12 << 20)),
        cost_estimate=pl.CostEstimate(flops=1, bytes_accessed=1, transcendentals=0),
    )(*weights, *inputs, *heads, *earlier)
    blocks, got = got[: plan.blocks], got[plan.blocks :]
    stream = None
    if not last:
        stream, got = got[0], got[1:]
    return blocks, stream, got


def shards(records, conv_weight, conv_bias, res_weight, skip_weight):
    record_count, rows, width = records.shape
    layers, taps = conv_weight.shape[:2]
    count, sections = lax.axis_size("tm"), lax.axis_size("segment")
    place, segment, core = lax.axis_index("tm"), lax.axis_index("segment"), lax.axis_index("chan")
    lags = [rows // 8, rows, rows * max(1, count // 8), rows * max(1, count // 2)]
    plan = Plan(count, sections, record_count)

    blocks = [
        lax.dynamic_index_in_dim(records, plan.record_at(lax.rem(place + turn, count)), 0, keepdims=False)
        for turn in range(count)
    ]
    for turn in range(1, count):
        blocks[turn] = lax.ppermute(blocks[turn], "tm", [(i, (i + turn) % count) for i in range(count)])
    conv = conv_weight.reshape(layers, taps, 2 * width)
    other_conv = swap_cores(conv_weight).reshape(layers, taps, 2 * width)
    weights = (conv, other_conv, conv_bias, swap_cores(conv_bias), res_weight, skip_weight, swap_cores(skip_weight))
    blocks[1], conv, other_conv = lax.optimization_barrier((blocks[1], conv, other_conv))
    weights = (conv, other_conv, *weights[2:])
    inputs = blocks + [swap_cores(jnp.concatenate(blocks, 0))]

    skips = {}
    fed = [inputs, inputs]
    for stage in range(sections):
        heads, crossed = (), []
        for half in range(2):
            earlier = []
            if stage == sections - 1:
                for index in range(plan.blocks):
                    members = plan.leave_groups(half, index)[0][1][1:]
                    if members:
                        block = skips[members[0]][index]
                        for member in members[1:]:
                            block = jnp.where(segment == member[0], skips[member][index], block)
                        earlier.append(block)
                earlier = earlier if len(earlier) == plan.blocks else []
            came = fed[half]
            if stage:
                if half:
                    came, heads = lax.optimization_barrier((came, heads))
                else:
                    came, stream = lax.optimization_barrier((came, stream))
                size = came.shape[0] // PIECES
                came = [came] + [swap_cores(came[i * size : (i + 1) * size]) for i in range(PIECES)]
            skips[stage, half], stream, carried = run_section(
                stage, half, plan, lags, weights, came, heads, earlier, rows
            )
            heads = carried
            if stage < sections - 1:
                moved = lax.ppermute(stream, "segment", [(i, (i + 1) % sections) for i in range(sections)])
                crossed.append(moved)
        fed = crossed

    arrived, holds = [], []
    spot = (place * sections + segment) * 2 + core

    def number(device):
        return (device[0] * sections + device[1]) * 2 + device[2]

    for phase in range(2):
        for index in range(plan.blocks):
            for sends, members in plan.leave_groups(phase, index):
                payload = skips[members[0]][index]
                if members[0][0] != sections - 1:
                    for member in members[1:]:
                        payload = jnp.where(segment == member[0], skips[member][index], payload)
                pairs = complete(sends, (count, sections, 2))
                arrived.append(
                    lax.ppermute(
                        payload, ("tm", "segment", "chan"), sorted((number(a), number(b)) for a, b in pairs.items())
                    )
                )
                if len(sends) < 2 * count * sections:
                    valid = functools.reduce(jnp.logical_or, [spot == number(d) for d in sends.values()])
                    holds.append(valid.astype(jnp.int32))
                else:
                    holds.append(1)
    masks = [] if all(isinstance(hold, int) for hold in holds) else [jnp.stack(holds)]
    kept, given = pl.pallas_call(
        functools.partial(sum_kernel, len(masks)),
        out_shape=[jax.ShapeDtypeStruct((rows, width), jnp.bfloat16)] * 2,
        in_specs=[pl.BlockSpec(memory_space=pltpu.SMEM)] * len(masks) + [VMEM] * len(arrived),
        out_specs=[VMEM] * 2,
        compiler_params=pltpu.CompilerParams(vmem_limit_bytes=4 << 20),
    )(*masks, *arrived)
    return pl.pallas_call(
        functools.partial(place_kernel, plan),
        out_shape=jax.ShapeDtypeStruct((plan.share, rows, width), jnp.bfloat16),
        in_specs=[VMEM] * 2,
        out_specs=VMEM,
        compiler_params=pltpu.CompilerParams(vmem_limit_bytes=4 << 20),
    )(kept, swap_cores(given))


def sum_kernel(masked, *refs):
    masks, arrived, (kept, given) = refs[:masked], refs[masked:-2], refs[-2:]
    width = kept.shape[1]
    core = lax.axis_index("chan")
    for side, out in ((core, kept), (1 - core, given)):
        lanes = pl.ds(pl.multiple_of(side * width, width), width)
        total = jnp.zeros(out.shape, jnp.float32)
        for index, block in enumerate(arrived):
            part = block[:, lanes].astype(jnp.float32)
            total += jnp.where(masks[0][index] == 1, part, 0.0) if masked else part
        out[...] = total.astype(out.dtype)


def place_kernel(plan, kept, given, out):
    half = lax.axis_index("tm") // (plan.count // 2)
    mine = lax.rem(lax.axis_index("chan") + half + lax.axis_index("segment") + 1, 2)
    for slot in range(plan.share):
        out[slot] = jnp.where(mine == slot, kept[...], given[...])


def solution(mesh):
    return jax.shard_map(
        shards,
        mesh=mesh,
        in_specs=(
            P("groups", "tm", "chan"),
            P("segment", None, None, "chan"),
            P("segment", None, "chan"),
            P("segment", None, None),
            P("segment", None, "chan"),
        ),
        out_specs=P(("groups", "segment"), "tm", "chan"),
        check_vma=False,
    )
```

```python
import functools

import jax
import jax.numpy as jnp
from jax import lax
from jax.experimental import pallas as pl
from jax.experimental.pallas import tpu as pltpu
from jax.sharding import PartitionSpec as P

VMEM = pl.BlockSpec(memory_space=pltpu.VMEM)
ROW_TILE = 512
PIECES = 2


class Plan:
    def __init__(self, count, sections, records):
        self.count, self.sections, self.records = count, sections, records
        self.share = records // sections
        self.whole_group = records <= count // 2
        self.blocks = records // 2 if self.whole_group else max(1, records // 4)

    def owner(self, z):
        return z % self.records % self.sections

    def slot(self, z):
        return z % self.records // self.sections

    def record_at(self, z):
        return self.owner(z) * self.share + self.slot(z)

    def time_block(self, z, core, half, index):
        if self.whole_group:
            return z // self.records * self.records + 2 * index + core
        return half * (self.count // 2) + 2 * index + core

    def landing_core(self, segment, half, slot):
        return (slot + half + segment + 1) % 2

    def from_chip(self, z, turn):
        return lax.rem(z - turn + self.count, self.count)

    def leave_groups(self, phase, index):
        groups = []
        for stage in reversed(range(self.sections)):
            half = phase if stage == self.sections - 1 else 1 - phase
            sends = self.transfers(stage, half, index)
            for known, members in groups:
                if not set(known.values()) & set(sends.values()):
                    known.update(sends)
                    members.append((stage, half))
                    break
            else:
                groups.append((sends, [(stage, half)]))
        return groups

    def transfers(self, stage, half, index):
        sends = {}
        for z in range(self.count):
            for core in range(2):
                t = self.time_block(z, core, half, index)
                if t // (self.count // 2) == half:
                    to = self.owner(z)
                    sends[z, stage, core] = (t, to, self.landing_core(to, half, self.slot(z)))
        return sends


def complete(sends, shape):
    devices = [(z, s, c) for z in range(shape[0]) for s in range(shape[1]) for c in range(shape[2])]
    taken = set(sends.values())
    sources = [d for d in devices if d not in sends]
    targets = [d for d in devices if d not in taken]
    pairs = dict(sends)

    def near(pair):
        a, b = pair
        return (a == b, abs(a[0] - b[0]), a[1] != b[1])

    for source in sources:
        target = min(targets, key=lambda b: near((source, b)))
        targets.remove(target)
        pairs[source] = target
    for a in [d for d in sources if pairs[d] == d]:
        b = next((d for d in sources if d != a and pairs[d] != a), None)
        if b is not None:
            pairs[a], pairs[b] = pairs[b], pairs[a]
    return pairs


def swap_cores(block):
    return lax.ppermute(block, "chan", [(0, 1), (1, 0)])


def section_kernel(stage, half, plan, lags, n_in, n_earlier, last, *refs):
    own_conv, other_conv, own_bias, other_bias, res_ref, own_skip, other_skip = refs[:7]
    inputs, refs = refs[7 : 7 + n_in], refs[7 + n_in :]
    layers, depth = res_ref.shape[:2]
    width = depth // 2
    heads = ()
    if half:
        heads, refs = refs[:layers], refs[layers:]
    earlier, refs = refs[:n_earlier], refs[n_earlier:]
    skip_outs, refs = refs[: plan.blocks], refs[plan.blocks :]
    if not last:
        stream_out, refs = refs[0], refs[1:]
    if not half:
        tails, refs = refs[:layers], refs[layers:]
    streams, units, out_buf = refs[:layers], refs[layers], refs[layers + 1]
    core, place = lax.axis_index("chan"), lax.axis_index("tm")
    total = units.shape[1]
    own_rows = pl.ds(pl.multiple_of(core * width, width), width)
    other_rows = pl.ds(pl.multiple_of((1 - core) * width, width), width)

    if earlier:

        @pl.when(lax.axis_index("segment") != stage)
        def _():
            for block, out in zip(earlier, skip_outs):
                out[...] = block[...]

    @pl.when(lax.axis_index("segment") == stage)
    def _():
        for layer in range(layers):
            lag = lags[layer % 4]
            streams[layer][:lag, :] = heads[layer][...] if half else jnp.zeros((lag, depth), jnp.bfloat16)
        if stage == 0:
            rows = inputs[0].shape[0]
            per_half = plan.count // 2
            for turn in range(plan.count):
                t = plan.from_chip(place, turn)

                @pl.when(t // per_half == half)
                def _(t=t, turn=turn):
                    at = pl.multiple_of(lags[0] + (t - half * per_half) * rows, 16)
                    streams[0][pl.ds(at, rows), own_rows] = inputs[turn][...]
                    streams[0][pl.ds(at, rows), other_rows] = inputs[plan.count][turn * rows : (turn + 1) * rows, :]
        else:
            part = inputs[0].shape[0]
            for piece, block in enumerate(inputs[1:]):
                size = block.shape[0]
                at = pl.multiple_of(lags[0] + (1 - core) * part + piece * size, 16)
                streams[0][pl.ds(at, size), :] = block[...]
            streams[0][pl.ds(pl.multiple_of(lags[0] + core * part, 16), part), :] = inputs[0][...]

        for layer in range(layers):
            lag = lags[layer % 4]
            now_buf = streams[layer]
            next_buf, next_lag = (streams[layer + 1], lags[(layer + 1) % 4]) if layer + 1 < layers else (out_buf, 0)
            res = None
            if not (last and layer + 1 == layers):
                res = jnp.concatenate([res_ref[layer, own_rows, :], res_ref[layer, other_rows, :]], 0)

            def tile(row, layer=layer, lag=lag, now_buf=now_buf, next_buf=next_buf, next_lag=next_lag, res=res):
                past = now_buf[pl.ds(row, ROW_TILE), :]
                now = now_buf[pl.ds(lag + row, ROW_TILE), :]
                parts = []
                both = jnp.concatenate([past, now], 1)
                for conv, bias in ((own_conv, own_bias), (other_conv, other_bias)):
                    shift = jnp.concatenate([bias[layer, 0:1, :], bias[layer, 1:2, :]], 1).astype(jnp.float32)
                    pre = jnp.dot(both, conv[layer], preferred_element_type=jnp.float32)
                    pre += shift
                    gate = 0.5 * jnp.tanh(0.5 * pre[:, width:]) + 0.5
                    parts.append((jnp.tanh(pre[:, :width]) * gate).astype(jnp.bfloat16))
                unit = jnp.concatenate(parts, 1)
                units[layer, pl.ds(row, ROW_TILE), :] = unit
                if res is not None:
                    update = jnp.dot(unit, res, preferred_element_type=jnp.float32)
                    next_buf[pl.ds(next_lag + row, ROW_TILE), :] = (now.astype(jnp.float32) + update).astype(jnp.bfloat16)

            steps = total // ROW_TILE
            if steps <= 4:
                for step in range(steps):
                    tile(step * ROW_TILE)
            else:
                pl.loop(0, steps)(lambda step: tile(pl.multiple_of(step * ROW_TILE, ROW_TILE)))

        if not last:
            part = total // 2
            stream_out[...] = out_buf[pl.ds(pl.multiple_of(core * part, 16), part), :]
        if not half:
            for layer in range(layers):
                tails[layer][...] = streams[layer][pl.ds(total, lags[layer % 4]), :]
        for index, out in enumerate(skip_outs):
            rows = out.shape[0]
            t = plan.time_block(place, core, half, index) - half * (plan.count // 2)
            at = pl.multiple_of(jnp.clip(t, 0, total // rows - 1) * rows, rows)
            acc = jnp.zeros((rows, depth), jnp.float32)
            for layer in range(layers):
                unit = units[layer, pl.ds(at, rows), :]
                skip = jnp.concatenate(
                    [
                        jnp.concatenate([part[layer, own_rows, :], part[layer, other_rows, :]], 0)
                        for part in (own_skip, other_skip)
                    ],
                    1,
                )
                acc += jnp.dot(unit, skip, preferred_element_type=jnp.float32)
            out[:, own_rows] = acc[:, :width].astype(out.dtype)
            out[:, other_rows] = acc[:, width:].astype(out.dtype)


def run_section(stage, half, plan, lags, weights, inputs, heads, earlier, rows):
    res_weight = weights[4]
    layers, depth = res_weight.shape[:2]
    total = rows * plan.count // 2
    last = stage == plan.sections - 1
    outs = [jax.ShapeDtypeStruct((rows, depth), jnp.bfloat16)] * plan.blocks
    if not last:
        outs.append(jax.ShapeDtypeStruct((total // 2, depth), jnp.bfloat16))
    if not half:
        outs += [jax.ShapeDtypeStruct((lags[layer % 4], depth), jnp.bfloat16) for layer in range(layers)]
    scratch = [pltpu.VMEM((lags[layer % 4] + total, depth), jnp.bfloat16) for layer in range(layers)]
    scratch += [pltpu.VMEM((layers, total, depth), jnp.bfloat16), pltpu.VMEM((total, depth), jnp.bfloat16)]
    held = 2 * depth * (sum(lags) * 3 + 13 * total)
    got = pl.pallas_call(
        functools.partial(section_kernel, stage, half, plan, lags, len(inputs), len(earlier), last),
        out_shape=outs,
        in_specs=[VMEM] * (len(weights) + len(inputs) + len(heads) + len(earlier)),
        out_specs=[VMEM] * len(outs),
        scratch_shapes=scratch,
        compiler_params=pltpu.CompilerParams(vmem_limit_bytes=held + (12 << 20)),
        cost_estimate=pl.CostEstimate(flops=1, bytes_accessed=1, transcendentals=0),
    )(*weights, *inputs, *heads, *earlier)
    blocks, got = got[: plan.blocks], got[plan.blocks :]
    stream = None
    if not last:
        stream, got = got[0], got[1:]
    return blocks, stream, got


def shards(records, conv_weight, conv_bias, res_weight, skip_weight):
    record_count, rows, width = records.shape
    layers, taps = conv_weight.shape[:2]
    count, sections = lax.axis_size("tm"), lax.axis_size("segment")
    place, segment, core = lax.axis_index("tm"), lax.axis_index("segment"), lax.axis_index("chan")
    lags = [rows // 8, rows, rows * max(1, count // 8), rows * max(1, count // 2)]
    plan = Plan(count, sections, record_count)

    blocks = [
        lax.dynamic_index_in_dim(records, plan.record_at(lax.rem(place + turn, count)), 0, keepdims=False)
        for turn in range(count)
    ]
    for turn in range(1, count):
        blocks[turn] = lax.ppermute(blocks[turn], "tm", [(i, (i + turn) % count) for i in range(count)])
    conv = conv_weight.reshape(layers, taps, 2 * width)
    other_conv = swap_cores(conv_weight).reshape(layers, taps, 2 * width)
    weights = (conv, other_conv, conv_bias, swap_cores(conv_bias), res_weight, skip_weight, swap_cores(skip_weight))
    blocks[1], conv, other_conv = lax.optimization_barrier((blocks[1], conv, other_conv))
    weights = (conv, other_conv, *weights[2:])
    inputs = blocks + [swap_cores(jnp.concatenate(blocks, 0))]

    skips = {}
    fed = [inputs, inputs]
    for stage in range(sections):
        heads, crossed = (), []
        for half in range(2):
            earlier = []
            if stage == sections - 1:
                for index in range(plan.blocks):
                    members = plan.leave_groups(half, index)[0][1][1:]
                    if members:
                        block = skips[members[0]][index]
                        for member in members[1:]:
                            block = jnp.where(segment == member[0], skips[member][index], block)
                        earlier.append(block)
                earlier = earlier if len(earlier) == plan.blocks else []
            came = fed[half]
            if stage:
                if half:
                    came, heads = lax.optimization_barrier((came, heads))
                else:
                    came, stream = lax.optimization_barrier((came, stream))
                size = came.shape[0] // PIECES
                came = [came] + [swap_cores(came[i * size : (i + 1) * size]) for i in range(PIECES)]
            skips[stage, half], stream, carried = run_section(
                stage, half, plan, lags, weights, came, heads, earlier, rows
            )
            heads = carried
            if stage < sections - 1:
                ring = [(i, (i + 1) % sections) for i in range(sections - half)]
                moved = lax.ppermute(stream, "segment", ring)
                crossed.append(moved)
        fed = crossed

    arrived, holds = [], []
    spot = (place * sections + segment) * 2 + core

    def number(device):
        return (device[0] * sections + device[1]) * 2 + device[2]

    for phase in range(2):
        for index in range(plan.blocks):
            for sends, members in plan.leave_groups(phase, index):
                payload = skips[members[0]][index]
                if members[0][0] != sections - 1:
                    for member in members[1:]:
                        payload = jnp.where(segment == member[0], skips[member][index], payload)
                pairs = complete(sends, (count, sections, 2))
                arrived.append(
                    lax.ppermute(
                        payload, ("tm", "segment", "chan"), sorted((number(a), number(b)) for a, b in pairs.items())
                    )
                )
                if len(sends) < 2 * count * sections:
                    valid = functools.reduce(jnp.logical_or, [spot == number(d) for d in sends.values()])
                    holds.append(valid.astype(jnp.int32))
                else:
                    holds.append(1)
    masks = [] if all(isinstance(hold, int) for hold in holds) else [jnp.stack(holds)]
    kept, given = pl.pallas_call(
        functools.partial(sum_kernel, len(masks)),
        out_shape=[jax.ShapeDtypeStruct((rows, width), jnp.bfloat16)] * 2,
        in_specs=[pl.BlockSpec(memory_space=pltpu.SMEM)] * len(masks) + [VMEM] * len(arrived),
        out_specs=[VMEM] * 2,
        compiler_params=pltpu.CompilerParams(vmem_limit_bytes=4 << 20),
    )(*masks, *arrived)
    return pl.pallas_call(
        functools.partial(place_kernel, plan),
        out_shape=jax.ShapeDtypeStruct((plan.share, rows, width), jnp.bfloat16),
        in_specs=[VMEM] * 2,
        out_specs=pl.BlockSpec(memory_space=pl.ANY),
        scratch_shapes=[pltpu.SemaphoreType.DMA((2,))],
        compiler_params=pltpu.CompilerParams(vmem_limit_bytes=4 << 20),
    )(kept, swap_cores(given))


def sum_kernel(masked, *refs):
    masks, arrived, (kept, given) = refs[:masked], refs[masked:-2], refs[-2:]
    width = kept.shape[1]
    core = lax.axis_index("chan")
    for side, out in ((core, kept), (1 - core, given)):
        lanes = pl.ds(pl.multiple_of(side * width, width), width)
        total = jnp.zeros(out.shape, jnp.float32)
        for index, block in enumerate(arrived):
            part = block[:, lanes].astype(jnp.float32)
            total += jnp.where(masks[0][index] == 1, part, 0.0) if masked else part
        out[...] = total.astype(out.dtype)


def place_kernel(plan, kept, given, out, sems):
    half = lax.axis_index("tm") // (plan.count // 2)
    mine = lax.rem(lax.axis_index("chan") + half + lax.axis_index("segment") + 1, 2)
    if plan.share == 2:
        copies = [
            pltpu.make_async_copy(kept, out.at[mine], sems.at[0]),
            pltpu.make_async_copy(given, out.at[1 - mine], sems.at[1]),
        ]
        for copy in copies:
            copy.start()
        for copy in copies:
            copy.wait()
    else:
        for when, part in ((mine == 0, kept), (mine != 0, given)):

            @pl.when(when)
            def _(part=part):
                copy = pltpu.make_async_copy(part, out.at[0], sems.at[0])
                copy.start()
                copy.wait()


def solution(mesh):
    return jax.shard_map(
        shards,
        mesh=mesh,
        in_specs=(
            P("groups", "tm", "chan"),
            P("segment", None, None, "chan"),
            P("segment", None, "chan"),
            P("segment", None, None),
            P("segment", None, "chan"),
        ),
        out_specs=P(("groups", "segment"), "tm", "chan"),
        check_vma=False,
    )
```

```python
import functools

import jax
import jax.numpy as jnp
from jax import lax
from jax.experimental import pallas as pl
from jax.experimental.pallas import tpu as pltpu
from jax.sharding import PartitionSpec as P

VMEM = pl.BlockSpec(memory_space=pltpu.VMEM)
ROW_TILE = 512
PIECES = 2


class Plan:
    def __init__(self, count, sections, records):
        self.count, self.sections, self.records = count, sections, records
        self.share = records // sections
        self.whole_group = records <= count // 2
        self.blocks = records // 2 if self.whole_group else max(1, records // 4)

    def owner(self, z):
        return z % self.records % self.sections

    def slot(self, z):
        return z % self.records // self.sections

    def record_at(self, z):
        return self.owner(z) * self.share + self.slot(z)

    def time_block(self, z, core, half, index):
        if self.whole_group:
            return z // self.records * self.records + 2 * index + core
        return half * (self.count // 2) + 2 * index + core

    def landing_core(self, segment, half, slot):
        return (slot + half + segment + 1) % 2

    def from_chip(self, z, turn):
        return lax.rem(z - turn + self.count, self.count)

    def leave_groups(self, phase, index):
        groups = []
        for stage in reversed(range(self.sections)):
            half = phase if stage == self.sections - 1 else 1 - phase
            sends = self.transfers(stage, half, index)
            for known, members in groups:
                if not set(known.values()) & set(sends.values()):
                    known.update(sends)
                    members.append((stage, half))
                    break
            else:
                groups.append((sends, [(stage, half)]))
        return groups

    def transfers(self, stage, half, index):
        sends = {}
        for z in range(self.count):
            for core in range(2):
                t = self.time_block(z, core, half, index)
                if t // (self.count // 2) == half:
                    to = self.owner(z)
                    sends[z, stage, core] = (t, to, self.landing_core(to, half, self.slot(z)))
        return sends


def complete(sends, shape):
    devices = [(z, s, c) for z in range(shape[0]) for s in range(shape[1]) for c in range(shape[2])]
    taken = set(sends.values())
    sources = [d for d in devices if d not in sends]
    targets = [d for d in devices if d not in taken]
    pairs = dict(sends)

    def near(pair):
        a, b = pair
        return (a == b, abs(a[0] - b[0]), a[1] != b[1])

    for source in sources:
        target = min(targets, key=lambda b: near((source, b)))
        targets.remove(target)
        pairs[source] = target
    for a in [d for d in sources if pairs[d] == d]:
        b = next((d for d in sources if d != a and pairs[d] != a), None)
        if b is not None:
            pairs[a], pairs[b] = pairs[b], pairs[a]
    return pairs


def swap_cores(block):
    return lax.ppermute(block, "chan", [(0, 1), (1, 0)])


def section_kernel(stage, half, plan, lags, n_in, n_earlier, last, *refs):
    own_conv, other_conv, own_bias, other_bias, res_ref, own_skip, other_skip = refs[:7]
    inputs, refs = refs[7 : 7 + n_in], refs[7 + n_in :]
    layers, depth = res_ref.shape[:2]
    width = depth // 2
    heads = ()
    if half:
        heads, refs = refs[:layers], refs[layers:]
    earlier, refs = refs[:n_earlier], refs[n_earlier:]
    skip_outs, refs = (refs[: plan.blocks], refs[plan.blocks :]) if last else (refs[:1], refs[1:])
    if not last:
        stream_out, refs = refs[0], refs[1:]
    if not half:
        tails, refs = refs[:layers], refs[layers:]
    streams, out_buf = refs[:layers], refs[layers]
    units = refs[layers + 1] if last else skip_outs[0]
    core, place = lax.axis_index("chan"), lax.axis_index("tm")
    total = units.shape[1]
    own_rows = pl.ds(pl.multiple_of(core * width, width), width)
    other_rows = pl.ds(pl.multiple_of((1 - core) * width, width), width)

    if earlier:

        @pl.when(lax.axis_index("segment") != stage)
        def _():
            for block, out in zip(earlier, skip_outs):
                out[...] = block[...]

    @pl.when(lax.axis_index("segment") == stage)
    def _():
        for layer in range(layers):
            lag = lags[layer % 4]
            streams[layer][:lag, :] = heads[layer][...] if half else jnp.zeros((lag, depth), jnp.bfloat16)
        if stage == 0:
            rows = inputs[0].shape[0]
            per_half = plan.count // 2
            for turn in range(plan.count):
                t = plan.from_chip(place, turn)

                @pl.when(t // per_half == half)
                def _(t=t, turn=turn):
                    at = pl.multiple_of(lags[0] + (t - half * per_half) * rows, 16)
                    streams[0][pl.ds(at, rows), own_rows] = inputs[turn][...]
                    streams[0][pl.ds(at, rows), other_rows] = inputs[plan.count][turn * rows : (turn + 1) * rows, :]
        else:
            part = inputs[0].shape[0]
            for piece, block in enumerate(inputs[1:]):
                size = block.shape[0]
                at = pl.multiple_of(lags[0] + (1 - core) * part + piece * size, 16)
                streams[0][pl.ds(at, size), :] = block[...]
            streams[0][pl.ds(pl.multiple_of(lags[0] + core * part, 16), part), :] = inputs[0][...]

        for layer in range(layers):
            lag = lags[layer % 4]
            now_buf = streams[layer]
            next_buf, next_lag = (streams[layer + 1], lags[(layer + 1) % 4]) if layer + 1 < layers else (out_buf, 0)
            res = None
            if not (last and layer + 1 == layers):
                res = jnp.concatenate([res_ref[layer, own_rows, :], res_ref[layer, other_rows, :]], 0)

            def tile(row, layer=layer, lag=lag, now_buf=now_buf, next_buf=next_buf, next_lag=next_lag, res=res):
                past = now_buf[pl.ds(row, ROW_TILE), :]
                now = now_buf[pl.ds(lag + row, ROW_TILE), :]
                parts = []
                both = jnp.concatenate([past, now], 1)
                for conv, bias in ((own_conv, own_bias), (other_conv, other_bias)):
                    shift = jnp.concatenate([bias[layer, 0:1, :], bias[layer, 1:2, :]], 1).astype(jnp.float32)
                    pre = jnp.dot(both, conv[layer], preferred_element_type=jnp.float32)
                    pre += shift
                    gate = 0.5 * jnp.tanh(0.5 * pre[:, width:]) + 0.5
                    parts.append((jnp.tanh(pre[:, :width]) * gate).astype(jnp.bfloat16))
                unit = jnp.concatenate(parts, 1)
                units[layer, pl.ds(row, ROW_TILE), :] = unit
                if res is not None:
                    update = jnp.dot(unit, res, preferred_element_type=jnp.float32)
                    next_buf[pl.ds(next_lag + row, ROW_TILE), :] = (now.astype(jnp.float32) + update).astype(jnp.bfloat16)

            steps = total // ROW_TILE
            if steps <= 4:
                for step in range(steps):
                    tile(step * ROW_TILE)
            else:
                pl.loop(0, steps)(lambda step: tile(pl.multiple_of(step * ROW_TILE, ROW_TILE)))

        if not last:
            part = total // 2
            stream_out[...] = out_buf[pl.ds(pl.multiple_of(core * part, 16), part), :]
        if not half:
            for layer in range(layers):
                tails[layer][...] = streams[layer][pl.ds(total, lags[layer % 4]), :]
        if last:
            emit(half, plan, units, own_skip, other_skip, skip_outs)


def emit(half, plan, units, own_skip, other_skip, skip_outs):
    core, place = lax.axis_index("chan"), lax.axis_index("tm")
    layers, total, depth = units.shape
    width = depth // 2
    own_rows = pl.ds(pl.multiple_of(core * width, width), width)
    other_rows = pl.ds(pl.multiple_of((1 - core) * width, width), width)
    for index, out in enumerate(skip_outs):
        rows = out.shape[0]
        t = plan.time_block(place, core, half, index) - half * (plan.count // 2)
        at = pl.multiple_of(jnp.clip(t, 0, total // rows - 1) * rows, rows)
        acc = jnp.zeros((rows, depth), jnp.float32)
        for layer in range(layers):
            unit = units[layer, pl.ds(at, rows), :]
            skip = jnp.concatenate(
                [
                    jnp.concatenate([part[layer, own_rows, :], part[layer, other_rows, :]], 0)
                    for part in (own_skip, other_skip)
                ],
                1,
            )
            acc += jnp.dot(unit, skip, preferred_element_type=jnp.float32)
        out[:, own_rows] = acc[:, :width].astype(out.dtype)
        out[:, other_rows] = acc[:, width:].astype(out.dtype)


def skip_kernel(stage, half, plan, own_skip, other_skip, units, *skip_outs):
    @pl.when(lax.axis_index("segment") == stage)
    def _():
        emit(half, plan, units, own_skip, other_skip, skip_outs)


def run_section(stage, half, plan, lags, weights, inputs, heads, earlier, rows):
    res_weight = weights[4]
    layers, depth = res_weight.shape[:2]
    total = rows * plan.count // 2
    last = stage == plan.sections - 1
    block_shapes = [jax.ShapeDtypeStruct((rows, depth), jnp.bfloat16)] * plan.blocks
    outs = list(block_shapes) if last else [jax.ShapeDtypeStruct((layers, total, depth), jnp.bfloat16)]
    if not last:
        outs.append(jax.ShapeDtypeStruct((total // 2, depth), jnp.bfloat16))
    if not half:
        outs += [jax.ShapeDtypeStruct((lags[layer % 4], depth), jnp.bfloat16) for layer in range(layers)]
    scratch = [pltpu.VMEM((lags[layer % 4] + total, depth), jnp.bfloat16) for layer in range(layers)]
    scratch.append(pltpu.VMEM((total, depth), jnp.bfloat16))
    if last:
        scratch.append(pltpu.VMEM((layers, total, depth), jnp.bfloat16))
    held = 2 * depth * (sum(lags) * 3 + 13 * total)
    got = pl.pallas_call(
        functools.partial(section_kernel, stage, half, plan, lags, len(inputs), len(earlier), last),
        out_shape=outs,
        in_specs=[VMEM] * (len(weights) + len(inputs) + len(heads) + len(earlier)),
        out_specs=[VMEM] * len(outs),
        scratch_shapes=scratch,
        compiler_params=pltpu.CompilerParams(vmem_limit_bytes=held + (12 << 20)),
        cost_estimate=pl.CostEstimate(flops=1, bytes_accessed=1, transcendentals=0),
    )(*weights, *inputs, *heads, *earlier)
    if last:
        blocks, got = got[: plan.blocks], got[plan.blocks :]
    else:
        blocks = pl.pallas_call(
            functools.partial(skip_kernel, stage, half, plan),
            out_shape=block_shapes,
            in_specs=[VMEM] * 3,
            out_specs=[VMEM] * plan.blocks,
            compiler_params=pltpu.CompilerParams(vmem_limit_bytes=held + (12 << 20)),
            cost_estimate=pl.CostEstimate(flops=1, bytes_accessed=1, transcendentals=0),
        )(*weights[5:7], got[0])
        got = got[1:]
    stream = None
    if not last:
        stream, got = got[0], got[1:]
    return blocks, stream, got


def shards(records, conv_weight, conv_bias, res_weight, skip_weight):
    record_count, rows, width = records.shape
    layers, taps = conv_weight.shape[:2]
    count, sections = lax.axis_size("tm"), lax.axis_size("segment")
    place, segment, core = lax.axis_index("tm"), lax.axis_index("segment"), lax.axis_index("chan")
    lags = [rows // 8, rows, rows * max(1, count // 8), rows * max(1, count // 2)]
    plan = Plan(count, sections, record_count)

    blocks = [
        lax.dynamic_index_in_dim(records, plan.record_at(lax.rem(place + turn, count)), 0, keepdims=False)
        for turn in range(count)
    ]
    for turn in range(1, count):
        blocks[turn] = lax.ppermute(blocks[turn], "tm", [(i, (i + turn) % count) for i in range(count)])
    conv = conv_weight.reshape(layers, taps, 2 * width)
    other_conv = swap_cores(conv_weight).reshape(layers, taps, 2 * width)
    weights = (conv, other_conv, conv_bias, swap_cores(conv_bias), res_weight, skip_weight, swap_cores(skip_weight))
    blocks[1], conv, other_conv = lax.optimization_barrier((blocks[1], conv, other_conv))
    weights = (conv, other_conv, *weights[2:])
    inputs = blocks + [swap_cores(jnp.concatenate(blocks, 0))]

    skips = {}
    fed = [inputs, inputs]
    for stage in range(sections):
        heads, crossed = (), []
        for half in range(2):
            earlier = []
            if stage == sections - 1:
                for index in range(plan.blocks):
                    members = plan.leave_groups(half, index)[0][1][1:]
                    if members:
                        block = skips[members[0]][index]
                        for member in members[1:]:
                            block = jnp.where(segment == member[0], skips[member][index], block)
                        earlier.append(block)
                earlier = earlier if len(earlier) == plan.blocks else []
            came = fed[half]
            if stage:
                if half:
                    came, heads = lax.optimization_barrier((came, heads))
                else:
                    came, stream = lax.optimization_barrier((came, stream))
                size = came.shape[0] // PIECES
                came = [came] + [swap_cores(came[i * size : (i + 1) * size]) for i in range(PIECES)]
            skips[stage, half], stream, carried = run_section(
                stage, half, plan, lags, weights, came, heads, earlier, rows
            )
            heads = carried
            if stage < sections - 1:
                ring = [(i, (i + 1) % sections) for i in range(sections - half)]
                moved = lax.ppermute(stream, "segment", ring)
                crossed.append(moved)
        fed = crossed

    arrived, holds = [], []
    spot = (place * sections + segment) * 2 + core

    def number(device):
        return (device[0] * sections + device[1]) * 2 + device[2]

    for phase in range(2):
        for index in range(plan.blocks):
            for sends, members in plan.leave_groups(phase, index):
                payload = skips[members[0]][index]
                if members[0][0] != sections - 1:
                    for member in members[1:]:
                        payload = jnp.where(segment == member[0], skips[member][index], payload)
                pairs = complete(sends, (count, sections, 2))
                arrived.append(
                    lax.ppermute(
                        payload, ("tm", "segment", "chan"), sorted((number(a), number(b)) for a, b in pairs.items())
                    )
                )
                if len(sends) < 2 * count * sections:
                    valid = functools.reduce(jnp.logical_or, [spot == number(d) for d in sends.values()])
                    holds.append(valid.astype(jnp.int32))
                else:
                    holds.append(1)
    masks = [] if all(isinstance(hold, int) for hold in holds) else [jnp.stack(holds)]
    kept, given = pl.pallas_call(
        functools.partial(sum_kernel, len(masks)),
        out_shape=[jax.ShapeDtypeStruct((rows, width), jnp.bfloat16)] * 2,
        in_specs=[pl.BlockSpec(memory_space=pltpu.SMEM)] * len(masks) + [VMEM] * len(arrived),
        out_specs=[VMEM] * 2,
        compiler_params=pltpu.CompilerParams(vmem_limit_bytes=4 << 20),
    )(*masks, *arrived)
    return pl.pallas_call(
        functools.partial(place_kernel, plan),
        out_shape=jax.ShapeDtypeStruct((plan.share, rows, width), jnp.bfloat16),
        in_specs=[VMEM] * 2,
        out_specs=pl.BlockSpec(memory_space=pl.ANY),
        scratch_shapes=[pltpu.SemaphoreType.DMA((2,))],
        compiler_params=pltpu.CompilerParams(vmem_limit_bytes=4 << 20),
    )(kept, swap_cores(given))


def sum_kernel(masked, *refs):
    masks, arrived, (kept, given) = refs[:masked], refs[masked:-2], refs[-2:]
    width = kept.shape[1]
    core = lax.axis_index("chan")
    for side, out in ((core, kept), (1 - core, given)):
        lanes = pl.ds(pl.multiple_of(side * width, width), width)
        total = jnp.zeros(out.shape, jnp.float32)
        for index, block in enumerate(arrived):
            part = block[:, lanes].astype(jnp.float32)
            total += jnp.where(masks[0][index] == 1, part, 0.0) if masked else part
        out[...] = total.astype(out.dtype)


def place_kernel(plan, kept, given, out, sems):
    half = lax.axis_index("tm") // (plan.count // 2)
    mine = lax.rem(lax.axis_index("chan") + half + lax.axis_index("segment") + 1, 2)
    if plan.share == 2:
        copies = [
            pltpu.make_async_copy(kept, out.at[mine], sems.at[0]),
            pltpu.make_async_copy(given, out.at[1 - mine], sems.at[1]),
        ]
        for copy in copies:
            copy.start()
        for copy in copies:
            copy.wait()
    else:
        for when, part in ((mine == 0, kept), (mine != 0, given)):

            @pl.when(when)
            def _(part=part):
                copy = pltpu.make_async_copy(part, out.at[0], sems.at[0])
                copy.start()
                copy.wait()


def solution(mesh):
    return jax.shard_map(
        shards,
        mesh=mesh,
        in_specs=(
            P("groups", "tm", "chan"),
            P("segment", None, None, "chan"),
            P("segment", None, "chan"),
            P("segment", None, None),
            P("segment", None, "chan"),
        ),
        out_specs=P(("groups", "segment"), "tm", "chan"),
        check_vma=False,
    )
```

```python
import functools

import jax
import jax.numpy as jnp
from jax import lax
from jax.experimental import pallas as pl
from jax.experimental.pallas import tpu as pltpu
from jax.sharding import PartitionSpec as P

VMEM = pl.BlockSpec(memory_space=pltpu.VMEM)
ROW_TILE = 512
PIECES = 2


class Plan:
    def __init__(self, count, sections, records):
        self.count, self.sections, self.records = count, sections, records
        self.share = records // sections
        self.whole_group = records <= count // 2
        self.blocks = records // 2 if self.whole_group else max(1, records // 4)

    def owner(self, z):
        return z % self.records % self.sections

    def slot(self, z):
        return z % self.records // self.sections

    def record_at(self, z):
        return self.owner(z) * self.share + self.slot(z)

    def time_block(self, z, core, half, index):
        if self.whole_group:
            return z // self.records * self.records + 2 * index + core
        return half * (self.count // 2) + 2 * index + core

    def landing_core(self, segment, half, slot):
        return (slot + half + segment + 1) % 2

    def from_chip(self, z, turn):
        return lax.rem(z - turn + self.count, self.count)

    def leave_groups(self, phase, index):
        groups = []
        for stage in reversed(range(self.sections)):
            half = phase if stage == self.sections - 1 else 1 - phase
            sends = self.transfers(stage, half, index)
            for known, members in groups:
                if not set(known.values()) & set(sends.values()):
                    known.update(sends)
                    members.append((stage, half))
                    break
            else:
                groups.append((sends, [(stage, half)]))
        return groups

    def transfers(self, stage, half, index):
        sends = {}
        for z in range(self.count):
            for core in range(2):
                t = self.time_block(z, core, half, index)
                if t // (self.count // 2) == half:
                    to = self.owner(z)
                    sends[z, stage, core] = (t, to, self.landing_core(to, half, self.slot(z)))
        return sends


def complete(sends, shape):
    devices = [(z, s, c) for z in range(shape[0]) for s in range(shape[1]) for c in range(shape[2])]
    taken = set(sends.values())
    sources = [d for d in devices if d not in sends]
    targets = [d for d in devices if d not in taken]
    pairs = dict(sends)

    def near(pair):
        a, b = pair
        return (a == b, abs(a[0] - b[0]), a[1] != b[1])

    for source in sources:
        target = min(targets, key=lambda b: near((source, b)))
        targets.remove(target)
        pairs[source] = target
    for a in [d for d in sources if pairs[d] == d]:
        b = next((d for d in sources if d != a and pairs[d] != a), None)
        if b is not None:
            pairs[a], pairs[b] = pairs[b], pairs[a]
    return pairs


def swap_cores(block):
    return lax.ppermute(block, "chan", [(0, 1), (1, 0)])


def section_kernel(stage, half, plan, lags, n_in, n_earlier, last, *refs):
    own_conv, other_conv, own_bias, other_bias, res_ref, own_skip, other_skip = refs[:7]
    inputs, refs = refs[7 : 7 + n_in], refs[7 + n_in :]
    layers, depth = res_ref.shape[:2]
    width = depth // 2
    heads = ()
    if half:
        heads, refs = refs[:layers], refs[layers:]
    earlier, refs = refs[:n_earlier], refs[n_earlier:]
    skip_outs, refs = (refs[: plan.blocks], refs[plan.blocks :]) if last else (refs[:1], refs[1:])
    if not last:
        stream_out, refs = refs[0], refs[1:]
    if not half:
        tails, refs = refs[:layers], refs[layers:]
    streams, out_buf = refs[:layers], refs[layers]
    units = refs[layers + 1] if last else skip_outs[0]
    core, place = lax.axis_index("chan"), lax.axis_index("tm")
    total = units.shape[1]
    own_rows = pl.ds(pl.multiple_of(core * width, width), width)
    other_rows = pl.ds(pl.multiple_of((1 - core) * width, width), width)

    if earlier:

        @pl.when(lax.axis_index("segment") != stage)
        def _():
            for block, out in zip(earlier, skip_outs):
                out[...] = block[...]

    @pl.when(lax.axis_index("segment") == stage)
    def _():
        for layer in range(layers):
            lag = lags[layer % 4]
            streams[layer][:lag, :] = heads[layer][...] if half else jnp.zeros((lag, depth), jnp.bfloat16)
        if stage == 0:
            rows = inputs[0].shape[0]
            per_half = plan.count // 2
            for turn in range(plan.count):
                t = plan.from_chip(place, turn)

                @pl.when(t // per_half == half)
                def _(t=t, turn=turn):
                    at = pl.multiple_of(lags[0] + (t - half * per_half) * rows, 16)
                    streams[0][pl.ds(at, rows), own_rows] = inputs[turn][...]
                    streams[0][pl.ds(at, rows), other_rows] = inputs[plan.count][turn * rows : (turn + 1) * rows, :]
        else:
            part = inputs[0].shape[0]
            for piece, block in enumerate(inputs[1:]):
                size = block.shape[0]
                at = pl.multiple_of(lags[0] + (1 - core) * part + piece * size, 16)
                streams[0][pl.ds(at, size), :] = block[...]
            streams[0][pl.ds(pl.multiple_of(lags[0] + core * part, 16), part), :] = inputs[0][...]

        for layer in range(layers):
            lag = lags[layer % 4]
            now_buf = streams[layer]
            next_buf, next_lag = (streams[layer + 1], lags[(layer + 1) % 4]) if layer + 1 < layers else (out_buf, 0)
            res = None
            if not (last and layer + 1 == layers):
                res = jnp.concatenate([res_ref[layer, own_rows, :], res_ref[layer, other_rows, :]], 0)

            def tile(row, layer=layer, lag=lag, now_buf=now_buf, next_buf=next_buf, next_lag=next_lag, res=res):
                past = now_buf[pl.ds(row, ROW_TILE), :]
                now = now_buf[pl.ds(lag + row, ROW_TILE), :]
                parts = []
                blank = not half and lag >= total
                both = now if blank else jnp.concatenate([past, now], 1)
                for conv, bias in ((own_conv, own_bias), (other_conv, other_bias)):
                    shift = jnp.concatenate([bias[layer, 0:1, :], bias[layer, 1:2, :]], 1).astype(jnp.float32)
                    pre = jnp.dot(both, conv[layer, depth if blank else 0 :], preferred_element_type=jnp.float32)
                    pre += shift
                    gate = 0.5 * jnp.tanh(0.5 * pre[:, width:]) + 0.5
                    parts.append((jnp.tanh(pre[:, :width]) * gate).astype(jnp.bfloat16))
                unit = jnp.concatenate(parts, 1)
                units[layer, pl.ds(row, ROW_TILE), :] = unit
                if res is not None:
                    update = jnp.dot(unit, res, preferred_element_type=jnp.float32)
                    next_buf[pl.ds(next_lag + row, ROW_TILE), :] = (now.astype(jnp.float32) + update).astype(jnp.bfloat16)

            steps = total // ROW_TILE
            if steps <= 4:
                for step in range(steps):
                    tile(step * ROW_TILE)
            else:
                pl.loop(0, steps)(lambda step: tile(pl.multiple_of(step * ROW_TILE, ROW_TILE)))

        if not last:
            part = total // 2
            stream_out[...] = out_buf[pl.ds(pl.multiple_of(core * part, 16), part), :]
        if not half:
            for layer in range(layers):
                tails[layer][...] = streams[layer][pl.ds(total, lags[layer % 4]), :]
        if last:
            emit(half, plan, units, own_skip, other_skip, skip_outs)


def emit(half, plan, units, own_skip, other_skip, skip_outs):
    core, place = lax.axis_index("chan"), lax.axis_index("tm")
    layers, total, depth = units.shape
    width = depth // 2
    own_rows = pl.ds(pl.multiple_of(core * width, width), width)
    other_rows = pl.ds(pl.multiple_of((1 - core) * width, width), width)
    for index, out in enumerate(skip_outs):
        rows = out.shape[0]
        t = plan.time_block(place, core, half, index) - half * (plan.count // 2)
        at = pl.multiple_of(jnp.clip(t, 0, total // rows - 1) * rows, rows)
        acc = jnp.zeros((rows, depth), jnp.float32)
        for layer in range(layers):
            unit = units[layer, pl.ds(at, rows), :]
            skip = jnp.concatenate(
                [
                    jnp.concatenate([part[layer, own_rows, :], part[layer, other_rows, :]], 0)
                    for part in (own_skip, other_skip)
                ],
                1,
            )
            acc += jnp.dot(unit, skip, preferred_element_type=jnp.float32)
        out[:, own_rows] = acc[:, :width].astype(out.dtype)
        out[:, other_rows] = acc[:, width:].astype(out.dtype)


def skip_kernel(stage, half, plan, own_skip, other_skip, units, *skip_outs):
    @pl.when(lax.axis_index("segment") == stage)
    def _():
        emit(half, plan, units, own_skip, other_skip, skip_outs)


def run_section(stage, half, plan, lags, weights, inputs, heads, earlier, rows):
    res_weight = weights[4]
    layers, depth = res_weight.shape[:2]
    total = rows * plan.count // 2
    last = stage == plan.sections - 1
    block_shapes = [jax.ShapeDtypeStruct((rows, depth), jnp.bfloat16)] * plan.blocks
    outs = list(block_shapes) if last else [jax.ShapeDtypeStruct((layers, total, depth), jnp.bfloat16)]
    if not last:
        outs.append(jax.ShapeDtypeStruct((total // 2, depth), jnp.bfloat16))
    if not half:
        outs += [jax.ShapeDtypeStruct((lags[layer % 4], depth), jnp.bfloat16) for layer in range(layers)]
    scratch = [pltpu.VMEM((lags[layer % 4] + total, depth), jnp.bfloat16) for layer in range(layers)]
    scratch.append(pltpu.VMEM((total, depth), jnp.bfloat16))
    if last:
        scratch.append(pltpu.VMEM((layers, total, depth), jnp.bfloat16))
    held = 2 * depth * (sum(lags) * 3 + 13 * total)
    got = pl.pallas_call(
        functools.partial(section_kernel, stage, half, plan, lags, len(inputs), len(earlier), last),
        out_shape=outs,
        in_specs=[VMEM] * (len(weights) + len(inputs) + len(heads) + len(earlier)),
        out_specs=[VMEM] * len(outs),
        scratch_shapes=scratch,
        compiler_params=pltpu.CompilerParams(vmem_limit_bytes=held + (12 << 20)),
        cost_estimate=pl.CostEstimate(flops=1, bytes_accessed=1, transcendentals=0),
    )(*weights, *inputs, *heads, *earlier)
    if last:
        blocks, got = got[: plan.blocks], got[plan.blocks :]
    else:
        blocks = pl.pallas_call(
            functools.partial(skip_kernel, stage, half, plan),
            out_shape=block_shapes,
            in_specs=[VMEM] * 3,
            out_specs=[VMEM] * plan.blocks,
            compiler_params=pltpu.CompilerParams(vmem_limit_bytes=held + (12 << 20)),
            cost_estimate=pl.CostEstimate(flops=1, bytes_accessed=1, transcendentals=0),
        )(*weights[5:7], got[0])
        got = got[1:]
    stream = None
    if not last:
        stream, got = got[0], got[1:]
    return blocks, stream, got


def shards(records, conv_weight, conv_bias, res_weight, skip_weight):
    record_count, rows, width = records.shape
    layers, taps = conv_weight.shape[:2]
    count, sections = lax.axis_size("tm"), lax.axis_size("segment")
    place, segment, core = lax.axis_index("tm"), lax.axis_index("segment"), lax.axis_index("chan")
    lags = [rows // 8, rows, rows * max(1, count // 8), rows * max(1, count // 2)]
    plan = Plan(count, sections, record_count)

    blocks = [
        lax.dynamic_index_in_dim(records, plan.record_at(lax.rem(place + turn, count)), 0, keepdims=False)
        for turn in range(count)
    ]
    for turn in range(1, count):
        blocks[turn] = lax.ppermute(blocks[turn], "tm", [(i, (i + turn) % count) for i in range(count)])
    conv = conv_weight.reshape(layers, taps, 2 * width)
    other_conv = swap_cores(conv_weight).reshape(layers, taps, 2 * width)
    weights = (conv, other_conv, conv_bias, swap_cores(conv_bias), res_weight, skip_weight, swap_cores(skip_weight))
    blocks[1], conv, other_conv = lax.optimization_barrier((blocks[1], conv, other_conv))
    weights = (conv, other_conv, *weights[2:])
    inputs = blocks + [swap_cores(jnp.concatenate(blocks, 0))]

    skips = {}
    fed = [inputs, inputs]
    for stage in range(sections):
        heads, crossed = (), []
        for half in range(2):
            earlier = []
            if stage == sections - 1:
                for index in range(plan.blocks):
                    members = plan.leave_groups(half, index)[0][1][1:]
                    if members:
                        block = skips[members[0]][index]
                        for member in members[1:]:
                            block = jnp.where(segment == member[0], skips[member][index], block)
                        earlier.append(block)
                earlier = earlier if len(earlier) == plan.blocks else []
            came = fed[half]
            if stage:
                if half:
                    came, heads = lax.optimization_barrier((came, heads))
                else:
                    came, stream = lax.optimization_barrier((came, stream))
                pieces = 1 if half else PIECES
                size = came.shape[0] // pieces
                came = [came] + [swap_cores(came[i * size : (i + 1) * size]) for i in range(pieces)]
            skips[stage, half], stream, carried = run_section(
                stage, half, plan, lags, weights, came, heads, earlier, rows
            )
            heads = carried
            if stage < sections - 1:
                ring = [(i, (i + 1) % sections) for i in range(sections - half)]
                moved = lax.ppermute(stream, "segment", ring)
                crossed.append(moved)
        fed = crossed

    arrived, holds = [], []
    spot = (place * sections + segment) * 2 + core

    def number(device):
        return (device[0] * sections + device[1]) * 2 + device[2]

    for phase in range(2):
        for index in range(plan.blocks):
            for sends, members in plan.leave_groups(phase, index):
                payload = skips[members[0]][index]
                if members[0][0] != sections - 1:
                    for member in members[1:]:
                        payload = jnp.where(segment == member[0], skips[member][index], payload)
                pairs = complete(sends, (count, sections, 2))
                arrived.append(
                    lax.ppermute(
                        payload, ("tm", "segment", "chan"), sorted((number(a), number(b)) for a, b in pairs.items())
                    )
                )
                if len(sends) < 2 * count * sections:
                    valid = functools.reduce(jnp.logical_or, [spot == number(d) for d in sends.values()])
                    holds.append(valid.astype(jnp.int32))
                else:
                    holds.append(1)
    masks = [] if all(isinstance(hold, int) for hold in holds) else [jnp.stack(holds)]
    kept, given = pl.pallas_call(
        functools.partial(sum_kernel, len(masks)),
        out_shape=[jax.ShapeDtypeStruct((rows, width), jnp.bfloat16)] * 2,
        in_specs=[pl.BlockSpec(memory_space=pltpu.SMEM)] * len(masks) + [VMEM] * len(arrived),
        out_specs=[VMEM] * 2,
        compiler_params=pltpu.CompilerParams(vmem_limit_bytes=4 << 20),
    )(*masks, *arrived)
    return pl.pallas_call(
        functools.partial(place_kernel, plan),
        out_shape=jax.ShapeDtypeStruct((plan.share, rows, width), jnp.bfloat16),
        in_specs=[VMEM] * 2,
        out_specs=pl.BlockSpec(memory_space=pl.ANY),
        scratch_shapes=[pltpu.SemaphoreType.DMA((2,))],
        compiler_params=pltpu.CompilerParams(vmem_limit_bytes=4 << 20),
    )(kept, swap_cores(given))


def sum_kernel(masked, *refs):
    masks, arrived, (kept, given) = refs[:masked], refs[masked:-2], refs[-2:]
    width = kept.shape[1]
    core = lax.axis_index("chan")
    for side, out in ((core, kept), (1 - core, given)):
        lanes = pl.ds(pl.multiple_of(side * width, width), width)
        total = jnp.zeros(out.shape, jnp.float32)
        for index, block in enumerate(arrived):
            part = block[:, lanes].astype(jnp.float32)
            total += jnp.where(masks[0][index] == 1, part, 0.0) if masked else part
        out[...] = total.astype(out.dtype)


def place_kernel(plan, kept, given, out, sems):
    half = lax.axis_index("tm") // (plan.count // 2)
    mine = lax.rem(lax.axis_index("chan") + half + lax.axis_index("segment") + 1, 2)
    if plan.share == 2:
        copies = [
            pltpu.make_async_copy(kept, out.at[mine], sems.at[0]),
            pltpu.make_async_copy(given, out.at[1 - mine], sems.at[1]),
        ]
        for copy in copies:
            copy.start()
        for copy in copies:
            copy.wait()
    else:
        for when, part in ((mine == 0, kept), (mine != 0, given)):

            @pl.when(when)
            def _(part=part):
                copy = pltpu.make_async_copy(part, out.at[0], sems.at[0])
                copy.start()
                copy.wait()


def solution(mesh):
    return jax.shard_map(
        shards,
        mesh=mesh,
        in_specs=(
            P("groups", "tm", "chan"),
            P("segment", None, None, "chan"),
            P("segment", None, "chan"),
            P("segment", None, None),
            P("segment", None, "chan"),
        ),
        out_specs=P(("groups", "segment"), "tm", "chan"),
        check_vma=False,
    )
```

```python
import functools

import jax
import jax.numpy as jnp
from jax import lax
from jax.experimental import pallas as pl
from jax.experimental.pallas import tpu as pltpu
from jax.sharding import PartitionSpec as P

VMEM = pl.BlockSpec(memory_space=pltpu.VMEM)
ROW_TILE = 512
PIECES = 2


class Plan:
    def __init__(self, count, sections, records):
        self.count, self.sections, self.records = count, sections, records
        self.share = records // sections
        self.whole_group = records <= count // 2
        self.blocks = records // 2 if self.whole_group else max(1, records // 4)

    def owner(self, z):
        return z % self.records % self.sections

    def slot(self, z):
        return z % self.records // self.sections

    def record_at(self, z):
        return self.owner(z) * self.share + self.slot(z)

    def time_block(self, z, core, half, index):
        if self.whole_group:
            return z // self.records * self.records + 2 * index + core
        return half * (self.count // 2) + 2 * index + core

    def landing_core(self, segment, half, slot):
        return (slot + half + segment + 1) % 2

    def from_chip(self, z, turn):
        return lax.rem(z - turn + self.count, self.count)

    def leave_groups(self, phase, index):
        groups = []
        for stage in reversed(range(self.sections)):
            half = phase if stage == self.sections - 1 else 1 - phase
            sends = self.transfers(stage, half, index)
            for known, members in groups:
                if not set(known.values()) & set(sends.values()):
                    known.update(sends)
                    members.append((stage, half))
                    break
            else:
                groups.append((sends, [(stage, half)]))
        return groups

    def transfers(self, stage, half, index):
        sends = {}
        for z in range(self.count):
            for core in range(2):
                t = self.time_block(z, core, half, index)
                if t // (self.count // 2) == half:
                    to = self.owner(z)
                    sends[z, stage, core] = (t, to, self.landing_core(to, half, self.slot(z)))
        return sends


def complete(sends, shape):
    devices = [(z, s, c) for z in range(shape[0]) for s in range(shape[1]) for c in range(shape[2])]
    taken = set(sends.values())
    sources = [d for d in devices if d not in sends]
    targets = [d for d in devices if d not in taken]
    pairs = dict(sends)

    def near(pair):
        a, b = pair
        return (a == b, abs(a[0] - b[0]), a[1] != b[1])

    for source in sources:
        target = min(targets, key=lambda b: near((source, b)))
        targets.remove(target)
        pairs[source] = target
    for a in [d for d in sources if pairs[d] == d]:
        b = next((d for d in sources if d != a and pairs[d] != a), None)
        if b is not None:
            pairs[a], pairs[b] = pairs[b], pairs[a]
    return pairs


def swap_cores(block):
    return lax.ppermute(block, "chan", [(0, 1), (1, 0)])


def section_kernel(stage, half, plan, lags, n_in, n_earlier, last, *refs):
    own_conv, other_conv, own_bias, other_bias, res_ref, own_skip, other_skip = refs[:7]
    inputs, refs = refs[7 : 7 + n_in], refs[7 + n_in :]
    layers, depth = res_ref.shape[:2]
    width = depth // 2
    heads = ()
    if half:
        heads, refs = refs[:layers], refs[layers:]
    earlier, refs = refs[:n_earlier], refs[n_earlier:]
    skip_outs, refs = (refs[: plan.blocks], refs[plan.blocks :]) if last else (refs[:1], refs[1:])
    if not last:
        stream_out, refs = refs[0], refs[1:]
    if not half:
        tails, refs = refs[:layers], refs[layers:]
    streams, out_buf = refs[:layers], refs[layers]
    units = refs[layers + 1] if last else skip_outs[0]
    core, place = lax.axis_index("chan"), lax.axis_index("tm")
    total = units.shape[1]
    own_rows = pl.ds(pl.multiple_of(core * width, width), width)
    other_rows = pl.ds(pl.multiple_of((1 - core) * width, width), width)

    if earlier:

        @pl.when(lax.axis_index("segment") != stage)
        def _():
            for block, out in zip(earlier, skip_outs):
                out[...] = block[...]

    @pl.when(lax.axis_index("segment") == stage)
    def _():
        for layer in range(layers):
            lag = lags[layer % 4]
            streams[layer][:lag, :] = heads[layer][...] if half else jnp.zeros((lag, depth), jnp.bfloat16)
        if stage == 0:
            rows = inputs[0].shape[0]
            per_half = plan.count // 2
            for turn in range(plan.count):
                t = plan.from_chip(place, turn)

                @pl.when(t // per_half == half)
                def _(t=t, turn=turn):
                    at = pl.multiple_of(lags[0] + (t - half * per_half) * rows, 16)
                    streams[0][pl.ds(at, rows), own_rows] = inputs[turn][...]
                    streams[0][pl.ds(at, rows), other_rows] = inputs[plan.count][turn * rows : (turn + 1) * rows, :]
        else:
            part = inputs[0].shape[0]
            for piece, block in enumerate(inputs[1:]):
                size = block.shape[0]
                at = pl.multiple_of(lags[0] + (1 - core) * part + piece * size, 16)
                streams[0][pl.ds(at, size), :] = block[...]
            streams[0][pl.ds(pl.multiple_of(lags[0] + core * part, 16), part), :] = inputs[0][...]

        narrow = last and plan.count == 4 and plan.blocks == 1 and not plan.whole_group and lags[(layers - 1) % 4] == total
        for layer in range(layers):
            lag = lags[layer % 4]
            now_buf = streams[layer]
            next_buf, next_lag = (streams[layer + 1], lags[(layer + 1) % 4]) if layer + 1 < layers else (out_buf, 0)
            res = None
            if not (last and layer + 1 == layers):
                res = jnp.concatenate([res_ref[layer, own_rows, :], res_ref[layer, other_rows, :]], 0)

            def tile(row, size=ROW_TILE, layer=layer, lag=lag, now_buf=now_buf, next_buf=next_buf, next_lag=next_lag, res=res):
                past = now_buf[pl.ds(row, size), :]
                now = now_buf[pl.ds(lag + row, size), :]
                parts = []
                blank = not half and lag >= total
                both = now if blank else jnp.concatenate([past, now], 1)
                for conv, bias in ((own_conv, own_bias), (other_conv, other_bias)):
                    shift = jnp.concatenate([bias[layer, 0:1, :], bias[layer, 1:2, :]], 1).astype(jnp.float32)
                    pre = jnp.dot(both, conv[layer, depth if blank else 0 :], preferred_element_type=jnp.float32)
                    pre += shift
                    gate = 0.5 * jnp.tanh(0.5 * pre[:, width:]) + 0.5
                    parts.append((jnp.tanh(pre[:, :width]) * gate).astype(jnp.bfloat16))
                unit = jnp.concatenate(parts, 1)
                units[layer, pl.ds(row, size), :] = unit
                if res is not None:
                    update = jnp.dot(unit, res, preferred_element_type=jnp.float32)
                    next_buf[pl.ds(next_lag + row, size), :] = (now.astype(jnp.float32) + update).astype(jnp.bfloat16)

            if narrow and layer >= layers - 2:
                tile(pl.multiple_of(core * (total // 2), 16), total // 2)
                continue
            steps = total // ROW_TILE
            if steps <= 4:
                for step in range(steps):
                    tile(step * ROW_TILE)
            else:
                pl.loop(0, steps)(lambda step: tile(pl.multiple_of(step * ROW_TILE, ROW_TILE)))

        if not last:
            part = total // 2
            stream_out[...] = out_buf[pl.ds(pl.multiple_of(core * part, 16), part), :]
        if not half:
            for layer in range(layers):
                tails[layer][...] = streams[layer][pl.ds(total, lags[layer % 4]), :]
        if last:
            emit(half, plan, units, own_skip, other_skip, skip_outs)


def emit(half, plan, units, own_skip, other_skip, skip_outs):
    core, place = lax.axis_index("chan"), lax.axis_index("tm")
    layers, total, depth = units.shape
    width = depth // 2
    own_rows = pl.ds(pl.multiple_of(core * width, width), width)
    other_rows = pl.ds(pl.multiple_of((1 - core) * width, width), width)
    for index, out in enumerate(skip_outs):
        rows = out.shape[0]
        t = plan.time_block(place, core, half, index) - half * (plan.count // 2)
        at = pl.multiple_of(jnp.clip(t, 0, total // rows - 1) * rows, rows)
        acc = jnp.zeros((rows, depth), jnp.float32)
        for layer in range(layers):
            unit = units[layer, pl.ds(at, rows), :]
            skip = jnp.concatenate(
                [
                    jnp.concatenate([part[layer, own_rows, :], part[layer, other_rows, :]], 0)
                    for part in (own_skip, other_skip)
                ],
                1,
            )
            acc += jnp.dot(unit, skip, preferred_element_type=jnp.float32)
        out[:, own_rows] = acc[:, :width].astype(out.dtype)
        out[:, other_rows] = acc[:, width:].astype(out.dtype)


def skip_kernel(stage, half, plan, own_skip, other_skip, units, *skip_outs):
    @pl.when(lax.axis_index("segment") == stage)
    def _():
        emit(half, plan, units, own_skip, other_skip, skip_outs)


def run_section(stage, half, plan, lags, weights, inputs, heads, earlier, rows):
    res_weight = weights[4]
    layers, depth = res_weight.shape[:2]
    total = rows * plan.count // 2
    last = stage == plan.sections - 1
    block_shapes = [jax.ShapeDtypeStruct((rows, depth), jnp.bfloat16)] * plan.blocks
    outs = list(block_shapes) if last else [jax.ShapeDtypeStruct((layers, total, depth), jnp.bfloat16)]
    if not last:
        outs.append(jax.ShapeDtypeStruct((total // 2, depth), jnp.bfloat16))
    if not half:
        outs += [jax.ShapeDtypeStruct((lags[layer % 4], depth), jnp.bfloat16) for layer in range(layers)]
    scratch = [pltpu.VMEM((lags[layer % 4] + total, depth), jnp.bfloat16) for layer in range(layers)]
    scratch.append(pltpu.VMEM((total, depth), jnp.bfloat16))
    if last:
        scratch.append(pltpu.VMEM((layers, total, depth), jnp.bfloat16))
    held = 2 * depth * (sum(lags) * 3 + 13 * total)
    got = pl.pallas_call(
        functools.partial(section_kernel, stage, half, plan, lags, len(inputs), len(earlier), last),
        out_shape=outs,
        in_specs=[VMEM] * (len(weights) + len(inputs) + len(heads) + len(earlier)),
        out_specs=[VMEM] * len(outs),
        scratch_shapes=scratch,
        compiler_params=pltpu.CompilerParams(vmem_limit_bytes=held + (12 << 20)),
        cost_estimate=pl.CostEstimate(flops=1, bytes_accessed=1, transcendentals=0),
    )(*weights, *inputs, *heads, *earlier)
    if last:
        blocks, got = got[: plan.blocks], got[plan.blocks :]
    else:
        blocks = pl.pallas_call(
            functools.partial(skip_kernel, stage, half, plan),
            out_shape=block_shapes,
            in_specs=[VMEM] * 3,
            out_specs=[VMEM] * plan.blocks,
            compiler_params=pltpu.CompilerParams(vmem_limit_bytes=held + (12 << 20)),
            cost_estimate=pl.CostEstimate(flops=1, bytes_accessed=1, transcendentals=0),
        )(*weights[5:7], got[0])
        got = got[1:]
    stream = None
    if not last:
        stream, got = got[0], got[1:]
    return blocks, stream, got


def shards(records, conv_weight, conv_bias, res_weight, skip_weight):
    record_count, rows, width = records.shape
    layers, taps = conv_weight.shape[:2]
    count, sections = lax.axis_size("tm"), lax.axis_size("segment")
    place, segment, core = lax.axis_index("tm"), lax.axis_index("segment"), lax.axis_index("chan")
    lags = [rows // 8, rows, rows * max(1, count // 8), rows * max(1, count // 2)]
    plan = Plan(count, sections, record_count)

    blocks = [
        lax.dynamic_index_in_dim(records, plan.record_at(lax.rem(place + turn, count)), 0, keepdims=False)
        for turn in range(count)
    ]
    for turn in range(1, count):
        blocks[turn] = lax.ppermute(blocks[turn], "tm", [(i, (i + turn) % count) for i in range(count)])
    conv = conv_weight.reshape(layers, taps, 2 * width)
    other_conv = swap_cores(conv_weight).reshape(layers, taps, 2 * width)
    weights = (conv, other_conv, conv_bias, swap_cores(conv_bias), res_weight, skip_weight, swap_cores(skip_weight))
    blocks[1], conv, other_conv = lax.optimization_barrier((blocks[1], conv, other_conv))
    weights = (conv, other_conv, *weights[2:])
    inputs = blocks + [swap_cores(jnp.concatenate(blocks, 0))]

    skips = {}
    fed = [inputs, inputs]
    for stage in range(sections):
        heads, crossed = (), []
        for half in range(2):
            earlier = []
            if stage == sections - 1:
                for index in range(plan.blocks):
                    members = plan.leave_groups(half, index)[0][1][1:]
                    if members:
                        block = skips[members[0]][index]
                        for member in members[1:]:
                            block = jnp.where(segment == member[0], skips[member][index], block)
                        earlier.append(block)
                earlier = earlier if len(earlier) == plan.blocks else []
            came = fed[half]
            if stage:
                if half:
                    came, heads = lax.optimization_barrier((came, heads))
                else:
                    came, stream = lax.optimization_barrier((came, stream))
                pieces = 1 if half else PIECES
                size = came.shape[0] // pieces
                came = [came] + [swap_cores(came[i * size : (i + 1) * size]) for i in range(pieces)]
            skips[stage, half], stream, carried = run_section(
                stage, half, plan, lags, weights, came, heads, earlier, rows
            )
            heads = carried
            if stage < sections - 1:
                ring = [(i, (i + 1) % sections) for i in range(sections - half)]
                moved = lax.ppermute(stream, "segment", ring)
                crossed.append(moved)
        fed = crossed

    arrived, holds = [], []
    spot = (place * sections + segment) * 2 + core

    def number(device):
        return (device[0] * sections + device[1]) * 2 + device[2]

    for phase in range(2):
        for index in range(plan.blocks):
            for sends, members in plan.leave_groups(phase, index):
                payload = skips[members[0]][index]
                if members[0][0] != sections - 1:
                    for member in members[1:]:
                        payload = jnp.where(segment == member[0], skips[member][index], payload)
                pairs = complete(sends, (count, sections, 2))
                arrived.append(
                    lax.ppermute(
                        payload, ("tm", "segment", "chan"), sorted((number(a), number(b)) for a, b in pairs.items())
                    )
                )
                if len(sends) < 2 * count * sections:
                    valid = functools.reduce(jnp.logical_or, [spot == number(d) for d in sends.values()])
                    holds.append(valid.astype(jnp.int32))
                else:
                    holds.append(1)
    masks = [] if all(isinstance(hold, int) for hold in holds) else [jnp.stack(holds)]
    kept, given = pl.pallas_call(
        functools.partial(sum_kernel, len(masks)),
        out_shape=[jax.ShapeDtypeStruct((rows, width), jnp.bfloat16)] * 2,
        in_specs=[pl.BlockSpec(memory_space=pltpu.SMEM)] * len(masks) + [VMEM] * len(arrived),
        out_specs=[VMEM] * 2,
        compiler_params=pltpu.CompilerParams(vmem_limit_bytes=4 << 20),
    )(*masks, *arrived)
    return pl.pallas_call(
        functools.partial(place_kernel, plan),
        out_shape=jax.ShapeDtypeStruct((plan.share, rows, width), jnp.bfloat16),
        in_specs=[VMEM] * 2,
        out_specs=pl.BlockSpec(memory_space=pl.ANY),
        scratch_shapes=[pltpu.SemaphoreType.DMA((2,))],
        compiler_params=pltpu.CompilerParams(vmem_limit_bytes=4 << 20),
    )(kept, swap_cores(given))


def sum_kernel(masked, *refs):
    masks, arrived, (kept, given) = refs[:masked], refs[masked:-2], refs[-2:]
    width = kept.shape[1]
    core = lax.axis_index("chan")
    for side, out in ((core, kept), (1 - core, given)):
        lanes = pl.ds(pl.multiple_of(side * width, width), width)
        total = jnp.zeros(out.shape, jnp.float32)
        for index, block in enumerate(arrived):
            part = block[:, lanes].astype(jnp.float32)
            total += jnp.where(masks[0][index] == 1, part, 0.0) if masked else part
        out[...] = total.astype(out.dtype)


def place_kernel(plan, kept, given, out, sems):
    half = lax.axis_index("tm") // (plan.count // 2)
    mine = lax.rem(lax.axis_index("chan") + half + lax.axis_index("segment") + 1, 2)
    if plan.share == 2:
        copies = [
            pltpu.make_async_copy(kept, out.at[mine], sems.at[0]),
            pltpu.make_async_copy(given, out.at[1 - mine], sems.at[1]),
        ]
        for copy in copies:
            copy.start()
        for copy in copies:
            copy.wait()
    else:
        for when, part in ((mine == 0, kept), (mine != 0, given)):

            @pl.when(when)
            def _(part=part):
                copy = pltpu.make_async_copy(part, out.at[0], sems.at[0])
                copy.start()
                copy.wait()


def solution(mesh):
    return jax.shard_map(
        shards,
        mesh=mesh,
        in_specs=(
            P("groups", "tm", "chan"),
            P("segment", None, None, "chan"),
            P("segment", None, "chan"),
            P("segment", None, None),
            P("segment", None, "chan"),
        ),
        out_specs=P(("groups", "segment"), "tm", "chan"),
        check_vma=False,
    )
```
